256 devices in a mesh: prow: 16 (over x, y_lo, core), pcol: 16 (over y_hi, z).
Axes of the slice: x: 4, y: 4 (y_hi: 2, y_lo: 2; y = y_hi * 2 + y_lo), z: 8, core: 2. Of those that a mesh axis runs over, the one named last changes fastest.
Arguments:
- g_top: float32 [2, 4096, 2, 4096], P(None, 'prow', None, 'pcol')
- l_one: float32 [2, 4096, 2048], P(None, 'prow', 'pcol'), may hold values from -0.9 to 0.9
- struct_one: int32 [8, 16], replicated, may hold values from 0 to 31, as said below
- dinv_one: float32 [256, 2048], P('prow', 'pcol'), may hold values from -3 to 3
- l_two: float32 [2, 4096, 2048], P(None, 'prow', 'pcol'), may hold values from -0.9 to 0.9
- lp_two: float32 [256, 2048], P(None, 'pcol'), may hold values from -0.36 to 0.36
- parent_two: int32 [8], replicated, may hold values from 0 to 7
- pos_two: int32 [8, 8], replicated, may hold values from 0 to 15, as said below
- dinv_two: float32 [256, 2048], P('prow', 'pcol'), may hold values from -3 to 3
Outputs:
- panel_one: float32 [2, 4096, 2048], P(None, 'prow', 'pcol')
- diag_one: float32 [256, 2048], P('prow', 'pcol')
- panel_two: float32 [2, 4096, 2048], P(None, 'prow', 'pcol')
- parent_rows: float32 [256, 2048], P('prow', 'pcol')
- diag_two: float32 [256, 2048], P('prow', 'pcol')
The draws below stay inside these ranges and needn't reach their ends.
Inputs may be any that keep to these rules, and one draw needn't show every extreme that they name: `struct_one`: each row holds 16 distinct top-separator block indices in increasing order. `pos_two`: each row holds 8 distinct positions in increasing order.
All inputs are finite; a program needn't handle non-finite values.
Results may differ from the reference program's by a relative error of at most 0.00012.
Values sent between devices are 32-bit elements; how exact they have to be, the bound alone decides.
No kernel may reach another device: no remote copies, remote signals or barrier semaphores. Data moves between devices by JAX's collectives and lax.ppermute only.
A program may use at most 128 MiB of HBM per device.

```python
import math
import jax
import jax.numpy as jnp
from jax import lax

BS = 256
MSUP = 8
NB = 32
NT = 8192
S1 = 16
S2 = 8
N_PROW = 16
N_PCOL = 16


def draw_g_top(key, part):
    key_base = jax.random.fold_in(key, 11)
    key_diag = jax.random.fold_in(key, 12)
    general = jax.random.normal(key_base, (NT, NT), jnp.float32) * (1.0 / math.sqrt(NT))
    diag_values = jax.random.uniform(key_diag, (NT,), jnp.float32, 1.0, 2.0)
    index_line = jnp.arange(NT)
    on_diag = (index_line[:, None] == index_line[None, :]).astype(jnp.float32)
    full = general + on_diag * diag_values[:, None]
    return full.reshape(NB // N_PROW, N_PROW * BS, NB // N_PCOL, N_PCOL * BS)


def sorted_subsets(key, rows_count, total, picked):
    keys = jax.random.split(key, rows_count)

    def one_row(row_key):
        return jnp.sort(jax.random.permutation(row_key, total)[:picked])
    return jax.vmap(one_row)(keys).astype(jnp.int32)


def draw_struct_one(key, part):
    return sorted_subsets(jax.random.fold_in(key, 21), MSUP, NB, S1)


def draw_pos_two(key, part):
    return sorted_subsets(jax.random.fold_in(key, 31), MSUP, S1, S2)


def draw_parent_two(key, part):
    key_vals = jax.random.fold_in(key, 41)
    key_order = jax.random.fold_in(key, 42)
    values = jax.random.randint(key_vals, (MSUP,), 0, MSUP).astype(jnp.int32)
    values = values.at[0].set(0).at[1].set(MSUP - 1)
    order_idx = jax.random.permutation(key_order, MSUP)
    return jnp.take(values, order_idx, axis=0).astype(jnp.int32)


def steps_of(key, extent, cuts, low, largest):
    factor_of, own = 1.0, jax.random.fold_in(key, 6)
    for axis_at, blocks in cuts:
        draws = jnp.exp(jax.random.uniform(jax.random.fold_in(own, axis_at), (blocks,), jnp.float32, low / len(cuts), largest / len(cuts)))
        factor_of = factor_of * jnp.repeat(draws, extent[axis_at] // blocks).reshape([-1 if axis == axis_at else 1 for axis in range(len(extent))])
    return factor_of


def scatter_about(rng, shape, width, bound, cuts=(), held_as=jnp.bfloat16):
    factor_of = steps_of(rng, shape, cuts, -0.22, 0.18) if cuts else 1.0
    drawn = jax.random.normal(rng, shape, jnp.float32) * width * factor_of
    return jnp.minimum(jnp.maximum(drawn, -bound), bound).astype(held_as)


def setup_inputs(seed: int = 0) -> dict:
    splits = jax.random.split(jax.random.key(seed), 10)
    g_top = draw_g_top(jax.random.fold_in(splits[9], 71), 0)
    l_one = scatter_about(splits[1], (NB // N_PROW, N_PROW * BS, MSUP * BS), 0.15, 0.9, ((1, 16), (2, 16)), jnp.float32)
    struct_one = draw_struct_one(jax.random.fold_in(splits[9], 71), 0)
    dinv_one = scatter_about(splits[3], (BS, MSUP * BS), 0.5, 3.0, ((0, 16), (1, 16)), jnp.float32)
    l_two = scatter_about(splits[4], (NB // N_PROW, N_PROW * BS, MSUP * BS), 0.15, 0.9, ((1, 16), (2, 16)), jnp.float32)
    lp_two = scatter_about(splits[5], (BS, MSUP * BS), 0.06, 0.36, ((1, 16),), jnp.float32)
    parent_two = draw_parent_two(jax.random.fold_in(splits[9], 71), 0)
    pos_two = draw_pos_two(jax.random.fold_in(splits[9], 71), 0)
    dinv_two = scatter_about(splits[8], (BS, MSUP * BS), 0.5, 3.0, ((0, 16), (1, 16)), jnp.float32)
    return dict(g_top=g_top, l_one=l_one, struct_one=struct_one, dinv_one=dinv_one, l_two=l_two, lp_two=lp_two, parent_two=parent_two, pos_two=pos_two, dinv_two=dinv_two)


def reference(g_top, l_one, struct_one, dinv_one, l_two, lp_two, parent_two, pos_two, dinv_two):
    exact_mode = lax.Precision.HIGHEST
    order_full = NB * BS
    ginv = g_top.reshape(order_full, order_full)
    blocks = jnp.arange(NB, dtype=jnp.int32)
    struct_two = jnp.take_along_axis(jnp.take(struct_one, parent_two, axis=0), pos_two, axis=1)

    def expand(struct_rows):
        flag_rows = jnp.any(struct_rows[None, :, :] == blocks[:, None, None], axis=2).astype(jnp.float32)
        return jnp.repeat(jnp.repeat(flag_rows, BS, axis=0), BS, axis=1)

    keep_one = expand(struct_one)
    keep_two = expand(struct_two)
    lm_one = l_one.reshape(order_full, MSUP * BS) * keep_one
    lm_two = l_two.reshape(order_full, MSUP * BS) * keep_two
    one_blocks = lm_one.reshape(order_full, MSUP, BS)
    parent_panel = jnp.take(one_blocks, parent_two, axis=1)
    lp_blocks = lp_two.reshape(BS, MSUP, BS)
    folded = lm_two.reshape(order_full, MSUP, BS) - jnp.einsum("rgb,bgc->rgc", parent_panel, lp_blocks, precision=exact_mode)
    inverse_one = -jnp.dot(ginv, lm_one, precision=exact_mode, preferred_element_type=jnp.float32)
    inverse_two = -jnp.dot(ginv, folded.reshape(order_full, MSUP * BS), precision=exact_mode, preferred_element_type=jnp.float32)
    panel_one = (inverse_one * keep_one).reshape(l_one.shape)
    panel_two = (inverse_two * keep_two).reshape(l_two.shape)
    inverse_one_blocks = inverse_one.reshape(order_full, MSUP, BS)
    inverse_two_blocks = inverse_two.reshape(order_full, MSUP, BS)
    diag_one = dinv_one - jnp.einsum("rkb,rkc->bkc", one_blocks, inverse_one_blocks, precision=exact_mode).reshape(BS, MSUP * BS)
    dinv_parents = jnp.take(dinv_one.reshape(BS, MSUP, BS), parent_two, axis=1)
    scaled = jnp.einsum("agb,bgc->agc", dinv_parents, lp_blocks, precision=exact_mode)
    parent_rows = -(jnp.einsum("rgb,rgc->bgc", parent_panel, inverse_two_blocks, precision=exact_mode) + scaled).reshape(BS, MSUP * BS)
    quad_term = jnp.einsum("agb,agc->bgc", lp_blocks, scaled, precision=exact_mode)
    fold_term = jnp.einsum("rgb,rgc->bgc", folded, inverse_two_blocks, precision=exact_mode)
    diag_two = dinv_two + (quad_term - fold_term).reshape(BS, MSUP * BS)
    return (panel_one, diag_one, panel_two, parent_rows, diag_two)
```

```python
import functools

import jax
import jax.numpy as jnp
from jax import lax
from jax.experimental import pallas as pl
from jax.experimental.pallas import tpu as pltpu
from jax.sharding import PartitionSpec as P

ROW_AXES = ("x", "y_lo", "core")
COL_AXES = ("y_hi", "z")
ALL_AXES = ROW_AXES + COL_AXES
exact = lax.Precision.HIGHEST


def split(a):
    hi = a.astype(jnp.bfloat16)
    return hi, (a - hi.astype(jnp.float32)).astype(jnp.bfloat16)


def dot3(a, b):
    f = functools.partial(jnp.dot, preferred_element_type=jnp.float32)
    return f(a[0], b[0]) + (f(a[0], b[1]) + f(a[1], b[0]))


def product_kernel(sc_ref, gh_ref, gl_ref, one_ref, two_ref, par_ref, lp_ref, out_ref):
    h = sc_ref[8]
    lp = jnp.concatenate(
        [jnp.concatenate([lp_ref[0, t], lp_ref[1, t]], axis=0) for t in range(2)], axis=1
    )
    lp = split(lp)
    acc = None
    for k in range(2):
        half = h if k == 0 else 1 - h
        one = jnp.concatenate([one_ref[half, 0], one_ref[half, 1]], axis=1)
        two = jnp.concatenate([two_ref[half, 0], two_ref[half, 1]], axis=1)
        par = jnp.concatenate([par_ref[half, 0], par_ref[half, 1]], axis=1)
        folded = two - dot3(split(par), lp)
        both = split(jnp.concatenate([one, folded], axis=1))
        term = dot3((gh_ref[k], gl_ref[k]), both)
        acc = term if acc is None else acc + term
    for level in range(2):
        for t in range(2):
            col = level * 256 + t * 128
            out_ref[t, level] = -acc[:, col : col + 128]


def product(scalars, g_hi, g_lo, gathered):
    rows = lambda n: (2, 2, n, 128)
    whole = pl.BlockSpec((2, 512, 512), lambda j, sc: (0, 0, 0))
    return pl.pallas_call(
        product_kernel,
        grid_spec=pltpu.PrefetchScalarGridSpec(
            num_scalar_prefetch=1,
            grid=(4,),
            in_specs=[
                whole,
                whole,
                pl.BlockSpec(rows(512), lambda j, sc: (0, j, 0, 0)),
                pl.BlockSpec(rows(512), lambda j, sc: (0, j, 1, 0)),
                pl.BlockSpec(rows(512), lambda j, sc: (0, sc[j], sc[4 + j], 0)),
                pl.BlockSpec(rows(128), lambda j, sc: (0, j, 12, 0)),
            ],
            out_specs=pl.BlockSpec((2, 2, 512, 128), lambda j, sc: (j, 0, 0, 0)),
        ),
        out_shape=jax.ShapeDtypeStruct((8, 2, 512, 128), jnp.float32),
        compiler_params=pltpu.CompilerParams(vmem_limit_bytes=48 * 2**20),
        cost_estimate=pl.CostEstimate(
            flops=8_000_000_000, bytes_accessed=24_000_000, transcendentals=0
        ),
    )(scalars, g_hi, g_lo, gathered, gathered, gathered, gathered)


def swap_pairs(flip):
    pairs = []
    for i in range(256):
        row, col = divmod(i, 16)
        pairs.append((i, (row // 8 * 8 + col % 8) * 16 + (col // 8 ^ flip) * 8 + row % 8))
    return pairs


def ring(n, step):
    return [(i, (i + step) % n) for i in range(n)]


def local(g_top, l_one, struct_one, dinv_one, l_two, lp_two, parent_two, pos_two, dinv_two):
    row = lax.axis_index(ROW_AXES)
    h = lax.axis_index("y_hi")
    z = lax.axis_index("z")
    mine = h * 4 + z // 2
    parent = parent_two[mine]

    blocks = jnp.arange(2, dtype=jnp.int32) * 16 + row
    list_one = lax.dynamic_index_in_dim(struct_one, mine, 0, keepdims=False)
    list_parent = lax.dynamic_index_in_dim(struct_one, parent, 0, keepdims=False)
    places = lax.dynamic_index_in_dim(pos_two, mine, 0, keepdims=False)
    picked = jnp.any(places[:, None] == jnp.arange(16)[None, :], axis=0)
    keep_one = jnp.any(list_one[None, :] == blocks[:, None], axis=1)[:, None, None]
    keep_two = jnp.any((list_parent[None, :] == blocks[:, None]) & picked[None, :], axis=1)
    keep_two = keep_two[:, None, None]
    one = jnp.where(keep_one, l_one, 0.0).reshape(512, 128)
    two = jnp.where(keep_two, l_two, 0.0).reshape(512, 128)

    lp_piece = lax.dynamic_slice_in_dim(lp_two, row // 8 * 128, 128, 0)
    near = lax.ppermute(jnp.concatenate([one, two, lp_piece]), ALL_AXES, swap_pairs(0))
    far = lax.ppermute(one, ALL_AXES, swap_pairs(1))
    payload = jnp.concatenate([near[:1024], far, near[1024:]])
    gathered = lax.all_gather(payload, ROW_AXES, axis=0, tiled=False)
    gathered = gathered.reshape(2, 8, 1664, 128)

    g_other = lax.ppermute(g_top, "y_hi", ring(2, 1))
    g = jnp.stack([g_top, g_other]).reshape(2, 512, 512)
    g_hi32 = lax.reduce_precision(g, 8, 7)
    g_hi = g_hi32.astype(jnp.bfloat16)
    g_lo = (g - g_hi32).astype(jnp.bfloat16)

    packed = jnp.concatenate([one, dinv_one])
    packed_far = lax.ppermute(packed, "y_hi", ring(2, 1))
    pair = jnp.stack([jnp.where(h == 0, packed, packed_far), jnp.where(h == 0, packed_far, packed)])
    pieces = {0: pair}
    right = left = pair
    for d in range(1, 5):
        right = lax.ppermute(right, "z", ring(8, 1))
        pieces[-d] = right
        if d < 4:
            left = lax.ppermute(left, "z", ring(8, -1))
            pieces[d] = left

    def fetch(super_index, part):
        want_h, want_z = super_index // 4, super_index % 4 * 2 + part
        total = jnp.zeros((528, 128), jnp.float32)
        for d, piece in pieces.items():
            for hh in range(2):
                hit = (want_h == hh) & (want_z == (z + d) % 8)
                total = jnp.where(hit, piece[hh], total)
        return total

    par = jnp.concatenate([fetch(parent, 0), fetch(parent, 1)], axis=1)
    sibling = z ^ 1
    one_next = jnp.where(sibling > z, pieces[1][h], pieces[-1][h])[:512]
    two_next = lax.ppermute(two, "z", [(i, i ^ 1) for i in range(8)])
    own_two = jnp.where(z % 2 == 0, jnp.concatenate([two, two_next], 1), jnp.concatenate([two_next, two], 1))
    own_one = jnp.where(z % 2 == 0, jnp.concatenate([one, one_next], 1), jnp.concatenate([one_next, one], 1))

    parents = lax.dynamic_slice_in_dim(parent_two, h * 4, 4, 0)
    place = jnp.where(parents // 4 == h, 0, 2)
    scalars = jnp.concatenate([parents % 4, place, h[None]]).astype(jnp.int32)
    partial = product(scalars, g_hi, g_lo, gathered)
    inverse = lax.psum_scatter(partial, "z", scatter_dimension=0, tiled=False)
    inv_one, inv_two = inverse[0], inverse[1]
    panel_one = jnp.where(keep_one, inv_one.reshape(2, 256, 128), 0.0)
    panel_two = jnp.where(keep_two, inv_two.reshape(2, 256, 128), 0.0)

    dot_t = lambda a, b: lax.dot_general(a, b, (((0,), (0,)), ((), ())), precision=exact)
    lp_pair = lax.dynamic_slice(gathered, (0, z // 2 * 2, 1536, 0), (2, 2, 128, 128))
    lp_own = lp_pair.transpose(0, 2, 1, 3).reshape(256, 256)
    scaled = jnp.dot(par[512:], lp_two, precision=exact)
    lp_slab = lax.dynamic_slice_in_dim(lp_own, row * 16, 16, 0)
    quad = dot_t(lp_slab, scaled)
    term_one = dot_t(own_one, inv_one)
    term_par = dot_t(par[:512], inv_two)
    term_two = quad - dot_t(own_two, inv_two) + dot_t(lp_own, term_par)
    terms = jnp.stack([term_one, term_par, term_two]).reshape(3, 16, 16, 128).transpose(1, 0, 2, 3)
    sums = jnp.sum(lax.all_to_all(terms, ROW_AXES, 0, 0), axis=0)
    diag_one = dinv_one - sums[0]
    parent_rows = -(sums[1] + scaled)
    diag_two = dinv_two + sums[2]
    return (panel_one, diag_one, panel_two, parent_rows, diag_two)


def solution(mesh):
    fine = jax.sharding.Mesh(mesh.devices.reshape(4, 2, 2, 2, 8), ALL_AXES)
    tall = P(None, ROW_AXES, COL_AXES)
    flat = P(ROW_AXES, COL_AXES)
    return jax.shard_map(
        local,
        mesh=fine,
        in_specs=(
            P(None, ROW_AXES, None, COL_AXES),
            tall,
            P(),
            flat,
            tall,
            P(None, COL_AXES),
            P(),
            P(),
            flat,
        ),
        out_specs=(tall, flat, tall, flat, flat),
        check_vma=False,
    )
```

```python
import functools

import jax
import jax.numpy as jnp
from jax import lax
from jax.experimental import pallas as pl
from jax.experimental.pallas import tpu as pltpu
from jax.sharding import PartitionSpec as P

ROW_AXES = ("x", "y_lo", "core")
COL_AXES = ("y_hi", "z")
ALL_AXES = ROW_AXES + COL_AXES
exact = lax.Precision.HIGHEST


def split(a):
    hi = a.astype(jnp.bfloat16)
    return hi, (a - hi.astype(jnp.float32)).astype(jnp.bfloat16)


def dot3(a, b):
    f = functools.partial(jnp.dot, preferred_element_type=jnp.float32)
    return f(a[0], b[0]) + (f(a[0], b[1]) + f(a[1], b[0]))


def one_kernel(sc_ref, gh_ref, gl_ref, one_ref, out_ref):
    h = sc_ref[0]
    acc = None
    for k in range(2):
        half = h if k == 0 else 1 - h
        one = jnp.concatenate([one_ref[half, 0, 0, 0], one_ref[half, 0, 0, 1]], axis=1)
        term = dot3((gh_ref[k], gl_ref[k]), split(one))
        acc = term if acc is None else acc + term
    out_ref[0] = -acc[:, :128]
    out_ref[1] = -acc[:, 128:]


def two_kernel(sc_ref, gh_ref, gl_ref, two_ref, par_ref, lp_ref, out_ref):
    h = sc_ref[0]
    lp = jnp.concatenate([lp_ref[0, 0, 0, 0], lp_ref[1, 0, 0, 0]], axis=0)
    lp = split(lp)
    acc = None
    for k in range(2):
        half = h if k == 0 else 1 - h
        par = jnp.concatenate([par_ref[half, 0, 0, 0], par_ref[half, 0, 0, 1]], axis=1)
        folded = two_ref[half, 0, 0, 0] - dot3(split(par), lp)
        term = dot3((gh_ref[k], gl_ref[k]), split(folded))
        acc = term if acc is None else acc + term
    out_ref[0] = -acc


WHOLE_G = pl.BlockSpec((2, 512, 512), lambda i, sc: (0, 0, 0))
PARAMS = pltpu.CompilerParams(vmem_limit_bytes=40 * 2**20)


def cost(slots, side):
    return pl.CostEstimate(
        flops=slots * 512 * (1024 + side) * 128 * 6,
        bytes_accessed=2**21 + slots * (2**20 + side * 4096),
        transcendentals=0,
    )


def product_one(h, g_hi, g_lo, gathered):
    return pl.pallas_call(
        one_kernel,
        grid_spec=pltpu.PrefetchScalarGridSpec(
            num_scalar_prefetch=1,
            grid=(4,),
            in_specs=[
                WHOLE_G,
                WHOLE_G,
                pl.BlockSpec((2, 1, 1, 2, 512, 128), lambda j, sc: (0, j // 2, sc[0], j % 2, 0, 0)),
            ],
            out_specs=pl.BlockSpec((2, 512, 128), lambda j, sc: (j, 0, 0)),
        ),
        out_shape=jax.ShapeDtypeStruct((8, 512, 128), jnp.float32),
        compiler_params=PARAMS,
        cost_estimate=cost(8, 0),
    )(h[None], g_hi, g_lo, gathered)


def product_two(h, slots, parents, g_hi, g_lo, gathered):
    n = slots.shape[0]
    scalars = jnp.concatenate([h[None], slots, parents]).astype(jnp.int32)
    par_map = lambda i, sc: (
        0,
        sc[1 + n + i] % 4 // 2,
        sc[1 + n + i] // 4,
        sc[1 + n + i] % 2,
        0,
        0,
    )
    return pl.pallas_call(
        two_kernel,
        grid_spec=pltpu.PrefetchScalarGridSpec(
            num_scalar_prefetch=1,
            grid=(n,),
            in_specs=[
                WHOLE_G,
                WHOLE_G,
                pl.BlockSpec(
                    (2, 1, 1, 1, 512, 128),
                    lambda i, sc: (0, sc[1 + i] // 4, sc[0], sc[1 + i] % 4, 1, 0),
                ),
                pl.BlockSpec((2, 1, 1, 2, 512, 128), par_map),
                pl.BlockSpec(
                    (2, 1, 1, 1, 128, 128),
                    lambda i, sc: (0, sc[1 + i] // 4, sc[0], sc[1 + i] % 4, 8, 0),
                ),
            ],
            out_specs=pl.BlockSpec((1, 512, 128), lambda i, sc: (i, 0, 0)),
        ),
        out_shape=jax.ShapeDtypeStruct((n, 512, 128), jnp.float32),
        compiler_params=PARAMS,
        cost_estimate=cost(n, 512),
    )(scalars, g_hi, g_lo, gathered, gathered, gathered)


def swap_pairs():
    pairs = []
    for i in range(256):
        row, col = divmod(i, 16)
        pairs.append((i, (row // 8 * 8 + col % 8) * 16 + col // 8 * 8 + row % 8))
    return pairs


def ring(n, step):
    return [(i, (i + step) % n) for i in range(n)]


def local(g_top, l_one, struct_one, dinv_one, l_two, lp_two, parent_two, pos_two, dinv_two):
    row = lax.axis_index(ROW_AXES)
    h = lax.axis_index("y_hi")
    z = lax.axis_index("z")
    mine = h * 4 + z // 2
    parent = parent_two[mine]

    blocks = jnp.arange(2, dtype=jnp.int32) * 16 + row
    list_one = lax.dynamic_index_in_dim(struct_one, mine, 0, keepdims=False)
    list_parent = lax.dynamic_index_in_dim(struct_one, parent, 0, keepdims=False)
    places = lax.dynamic_index_in_dim(pos_two, mine, 0, keepdims=False)
    picked = jnp.any(places[:, None] == jnp.arange(16)[None, :], axis=0)
    keep_one = jnp.any(list_one[None, :] == blocks[:, None], axis=1)[:, None, None]
    keep_two = jnp.any((list_parent[None, :] == blocks[:, None]) & picked[None, :], axis=1)
    keep_two = keep_two[:, None, None]
    one = jnp.where(keep_one, l_one, 0.0).reshape(512, 128)
    two = jnp.where(keep_two, l_two, 0.0).reshape(512, 128)

    lp_piece = lax.dynamic_slice_in_dim(lp_two, row // 8 * 128, 128, 0)
    near = lax.ppermute(jnp.concatenate([one, two, lp_piece]), ALL_AXES, swap_pairs())
    near, g_top, packed, two_sent = lax.optimization_barrier(
        (near, g_top, jnp.concatenate([one, dinv_one]), two)
    )
    gathered = lax.all_gather(near, ("x", "y_hi", "y_lo", "core"), axis=0, tiled=False)
    gathered = gathered.reshape(2, 2, 2, 4, 1152, 128)

    g_other = lax.ppermute(g_top, "y_hi", ring(2, 1))
    g = jnp.stack([g_top, g_other]).reshape(2, 512, 512)
    g_hi32 = lax.reduce_precision(g, 8, 7)
    g_hi = g_hi32.astype(jnp.bfloat16)
    g_lo = (g - g_hi32).astype(jnp.bfloat16)

    packed_far = lax.ppermute(packed, "y_hi", ring(2, 1))
    pair = jnp.stack([jnp.where(h == 0, packed, packed_far), jnp.where(h == 0, packed_far, packed)])
    pieces = {0: pair}
    right = left = pair
    for d in range(1, 5):
        right = lax.ppermute(right, "z", ring(8, 1))
        pieces[-d] = right
        if d < 4:
            left = lax.ppermute(left, "z", ring(8, -1))
            pieces[d] = left

    def fetch(super_index, part):
        want_h, want_z = super_index // 4, super_index % 4 * 2 + part
        total = jnp.zeros((528, 128), jnp.float32)
        for d, piece in pieces.items():
            for hh in range(2):
                hit = (want_h == hh) & (want_z == (z + d) % 8)
                total = jnp.where(hit, piece[hh], total)
        return total

    par = jnp.concatenate([fetch(parent, 0), fetch(parent, 1)], axis=1)
    sibling = z ^ 1
    one_next = jnp.where(sibling > z, pieces[1][h], pieces[-1][h])[:512]
    two_next = lax.ppermute(two_sent, "z", [(i, i ^ 1) for i in range(8)])
    own_two = jnp.where(z % 2 == 0, jnp.concatenate([two, two_next], 1), jnp.concatenate([two_next, two], 1))
    own_one = jnp.where(z % 2 == 0, jnp.concatenate([one, one_next], 1), jnp.concatenate([one_next, one], 1))

    h_now, par, own_one, own_two = lax.optimization_barrier((h, par, own_one, own_two))
    part_one = product_one(h_now, g_hi, g_lo, gathered)
    inv_one = lax.psum_scatter(part_one, "z", scatter_dimension=0, tiled=False)

    def level_two(steps, h_in):
        slots = (z + jnp.array(steps, jnp.int32)) % 8
        parents = jnp.take(parent_two, h * 4 + slots // 2)
        return product_two(h_in, slots, parents, g_hi, g_lo, gathered)

    h_next, part_one = lax.optimization_barrier((h_now, part_one[0, :8]))
    first = level_two((4, 5), h_next)
    h_last, first = lax.optimization_barrier((h_next, first))
    rest = level_two((3, 6, 2, 7, 1, 0), h_last)
    up, down = first[0], first[1]
    for d in range(3):
        up = lax.ppermute(up, "z", ring(8, 1)) + rest[2 * d]
        down = lax.ppermute(down, "z", ring(8, -1))
        if d < 2:
            down = down + rest[2 * d + 1]
    inv_two = lax.ppermute(up, "z", ring(8, 1)) + down + rest[5]
    panel_one = jnp.where(keep_one, inv_one.reshape(2, 256, 128), 0.0)
    panel_two = jnp.where(keep_two, inv_two.reshape(2, 256, 128), 0.0)

    dot_t = lambda a, b: lax.dot_general(a, b, (((0,), (0,)), ((), ())), precision=exact)
    lp_pair = lax.dynamic_slice(
        gathered, (0, z // 4, h, z % 4 // 2 * 2, 1024, 0), (2, 1, 1, 2, 128, 128)
    )
    lp_own = lp_pair.reshape(2, 2, 128, 128).transpose(0, 2, 1, 3).reshape(256, 256)
    scaled = jnp.dot(par[512:], lp_two, precision=exact)
    lp_slab = lax.dynamic_slice_in_dim(lp_own, row * 16, 16, 0)
    quad = dot_t(lp_slab, scaled)
    term_one = dot_t(own_one, inv_one)
    term_par = dot_t(par[:512], inv_two)
    term_two = quad - dot_t(own_two, inv_two) + dot_t(lp_own, term_par)
    terms = jnp.stack([term_one, term_par, term_two]).reshape(3, 16, 16, 128).transpose(1, 0, 2, 3)
    sums = jnp.sum(lax.all_to_all(terms, ROW_AXES, 0, 0), axis=0)
    diag_one = dinv_one - sums[0]
    parent_rows = -(sums[1] + scaled)
    diag_two = dinv_two + sums[2]
    return (panel_one, diag_one, panel_two, parent_rows, diag_two)


def solution(mesh):
    fine = jax.sharding.Mesh(mesh.devices.reshape(4, 2, 2, 2, 8), ALL_AXES)
    tall = P(None, ROW_AXES, COL_AXES)
    flat = P(ROW_AXES, COL_AXES)
    return jax.shard_map(
        local,
        mesh=fine,
        in_specs=(
            P(None, ROW_AXES, None, COL_AXES),
            tall,
            P(),
            flat,
            tall,
            P(None, COL_AXES),
            P(),
            P(),
            flat,
        ),
        out_specs=(tall, flat, tall, flat, flat),
        check_vma=False,
    )
```

```python
import functools

import jax
import jax.numpy as jnp
from jax import lax
from jax.experimental import pallas as pl
from jax.experimental.pallas import tpu as pltpu
from jax.sharding import PartitionSpec as P

ROW_AXES = ("x", "y_lo", "core")
COL_AXES = ("y_hi", "z")
ALL_AXES = ROW_AXES + COL_AXES
exact = lax.Precision.HIGHEST


def split(a):
    hi = a.astype(jnp.bfloat16)
    return hi, (a - hi.astype(jnp.float32)).astype(jnp.bfloat16)


def dot3(a, b):
    f = functools.partial(jnp.dot, preferred_element_type=jnp.float32)
    return f(a[0], b[0]) + (f(a[0], b[1]) + f(a[1], b[0]))


def one_kernel(sc_ref, gh_ref, gl_ref, a_ref, b_ref, out_ref):
    h = sc_ref[0]
    acc = None
    for k in range(2):
        half = h if k == 0 else 1 - h
        one = jnp.concatenate([a_ref[half, 0, 0, 0], b_ref[half, 0, 0, 0]], axis=1)
        term = dot3((gh_ref[k], gl_ref[k]), split(one))
        acc = term if acc is None else acc + term
    out_ref[0] = -acc[:, :128]
    out_ref[1] = -acc[:, 128:]


def two_kernel(sc_ref, gh_ref, gl_ref, a_ref, b_ref, pa_ref, pb_ref, la_ref, lb_ref, out_ref):
    h = sc_ref[0]
    lp = jnp.concatenate(
        [jnp.concatenate([r[0, 0, 0, 0], r[1, 0, 0, 0]], axis=0) for r in (la_ref, lb_ref)], axis=1
    )
    lp = split(lp)
    acc = None
    for k in range(2):
        half = h if k == 0 else 1 - h
        two = jnp.concatenate([a_ref[half, 0, 0, 0], b_ref[half, 0, 0, 0]], axis=1)
        par = jnp.concatenate([pa_ref[half, 0, 0, 0], pb_ref[half, 0, 0, 0]], axis=1)
        folded = two - dot3(split(par), lp)
        term = dot3((gh_ref[k], gl_ref[k]), split(folded))
        acc = term if acc is None else acc + term
    out_ref[0] = -acc[:, :128]
    out_ref[1] = -acc[:, 128:]


WHOLE_G = pl.BlockSpec((2, 512, 512), lambda i, sc: (0, 0, 0))
PARAMS = pltpu.CompilerParams(vmem_limit_bytes=40 * 2**20)


def piece(rows, block, first, stride):
    def place(i, sc):
        code = sc[first + stride * i]
        return (0, code // 8, code // 4 % 2, code % 4, block, 0)

    return pl.BlockSpec((2, 1, 1, 1, rows, 128), place)


def product(kernel, pieces, flops, scalars, pairs, g_hi, g_lo, gathered):
    return pl.pallas_call(
        kernel,
        grid_spec=pltpu.PrefetchScalarGridSpec(
            num_scalar_prefetch=1,
            grid=(pairs,),
            in_specs=[WHOLE_G, WHOLE_G, *pieces],
            out_specs=pl.BlockSpec((2, 512, 128), lambda i, sc: (i, 0, 0)),
        ),
        out_shape=jax.ShapeDtypeStruct((2 * pairs, 512, 128), jnp.float32),
        compiler_params=PARAMS,
        cost_estimate=pl.CostEstimate(
            flops=pairs * flops, bytes_accessed=pairs * 4_000_000, transcendentals=0
        ),
    )(scalars, g_hi, g_lo, *[gathered] * len(pieces))


product_one = functools.partial(
    product, one_kernel, [piece(512, 0, 1 + t, 2) for t in range(2)], 800_000_000
)
product_two = functools.partial(
    product,
    two_kernel,
    [piece(512, 1, 1 + t, 4) for t in range(2)]
    + [piece(512, 0, 3 + t, 4) for t in range(2)]
    + [piece(128, 8, 1 + t, 4) for t in range(2)],
    1_600_000_000,
)


def chip_and_core(shift):
    up = (shift >= 1) & (shift <= 4)
    return (up * (4 - shift) + (1 - up) * (8 - shift)) % 4, 1 - up


def spread_pairs(sign):
    pairs = []
    for i in range(256):
        row, col = divmod(i, 16)
        half, z, h, s = row // 8, row % 8, col // 8, col % 8
        chip, core = chip_and_core(sign * (z - s) % 8)
        pairs.append((i, (half * 8 + chip * 2 + int(core)) * 16 + h * 8 + z))
    return pairs


def ring(n, step):
    return [(i, (i + step) % n) for i in range(n)]


def local(g_top, l_one, struct_one, dinv_one, l_two, lp_two, parent_two, pos_two, dinv_two):
    row = lax.axis_index(ROW_AXES)
    h = lax.axis_index("y_hi")
    z = lax.axis_index("z")
    mine = h * 4 + z // 2
    parent = parent_two[mine]

    blocks = jnp.arange(2, dtype=jnp.int32) * 16 + row
    list_one = lax.dynamic_index_in_dim(struct_one, mine, 0, keepdims=False)
    list_parent = lax.dynamic_index_in_dim(struct_one, parent, 0, keepdims=False)
    places = lax.dynamic_index_in_dim(pos_two, mine, 0, keepdims=False)
    picked = jnp.any(places[:, None] == jnp.arange(16)[None, :], axis=0)
    keep_one = jnp.any(list_one[None, :] == blocks[:, None], axis=1)[:, None, None]
    keep_two = jnp.any((list_parent[None, :] == blocks[:, None]) & picked[None, :], axis=1)
    keep_two = keep_two[:, None, None]
    one = jnp.where(keep_one, l_one, 0.0).reshape(512, 128)
    two = jnp.where(keep_two, l_two, 0.0).reshape(512, 128)

    lp_piece = lax.dynamic_slice_in_dim(lp_two, row // 8 * 128, 128, 0)
    near_one = lax.ppermute(one, ALL_AXES, spread_pairs(1))
    near_two = lax.ppermute(jnp.concatenate([two, lp_piece]), ALL_AXES, spread_pairs(-1))
    packed = jnp.concatenate([one, dinv_one])
    packed_far = lax.ppermute(packed, "y_hi", ring(2, 1))
    g_other = lax.ppermute(g_top, "y_hi", ring(2, 1))
    near_one, near_two, packed, packed_far, two_sent, g_other = lax.optimization_barrier(
        (near_one, near_two, packed, packed_far, two, g_other)
    )
    near = jnp.concatenate([near_one, near_two])
    gathered = lax.all_gather(near, ("x", "y_hi", "y_lo", "core"), axis=0, tiled=False)
    gathered = gathered.reshape(2, 2, 2, 4, 1152, 128)

    def place(slot, sign):
        chip, core = chip_and_core(sign * (z - slot) % 8)
        return chip // 2 * 8 + slot // 8 * 4 + chip % 2 * 2 + core

    g = jnp.stack([g_top, g_other]).reshape(2, 512, 512)
    g_hi32 = lax.reduce_precision(g, 8, 7)
    g_hi = g_hi32.astype(jnp.bfloat16)
    g_lo = (g - g_hi32).astype(jnp.bfloat16)

    pair = jnp.stack([jnp.where(h == 0, packed, packed_far), jnp.where(h == 0, packed_far, packed)])
    pieces = {0: pair}
    right = left = pair
    for d in range(1, 5):
        right = lax.ppermute(right, "z", ring(8, 1))
        pieces[-d] = right
        if d < 4:
            left = lax.ppermute(left, "z", ring(8, -1))
            pieces[d] = left

    def fetch(super_index, part):
        want_h, want_z = super_index // 4, super_index % 4 * 2 + part
        total = jnp.zeros((528, 128), jnp.float32)
        for d, piece in pieces.items():
            for hh in range(2):
                hit = (want_h == hh) & (want_z == (z + d) % 8)
                total = jnp.where(hit, piece[hh], total)
        return total

    par = jnp.concatenate([fetch(parent, 0), fetch(parent, 1)], axis=1)
    sibling = z ^ 1
    one_next = jnp.where(sibling > z, pieces[1][h], pieces[-1][h])[:512]
    two_next = lax.ppermute(two_sent, "z", [(i, i ^ 1) for i in range(8)])
    own_two = jnp.where(z % 2 == 0, jnp.concatenate([two, two_next], 1), jnp.concatenate([two_next, two], 1))
    own_one = jnp.where(z % 2 == 0, jnp.concatenate([one, one_next], 1), jnp.concatenate([one_next, one], 1))

    slots = h * 8 + jnp.arange(8, dtype=jnp.int32)
    h_now, par, own_one, own_two = lax.optimization_barrier((h, par, own_one, own_two))
    scalars = jnp.concatenate([h_now[None], place(slots, 1)]).astype(jnp.int32)
    part_one = product_one(scalars, 4, g_hi, g_lo, gathered)
    inv_one = lax.psum_scatter(part_one, "z", scatter_dimension=0, tiled=False)

    def level_two(first_pair, h_in):
        supers = h * 4 + (first_pair + jnp.arange(2, dtype=jnp.int32)) % 4
        parents = parent_two.at[supers].get(mode="promise_in_bounds")
        two_slots = supers[:, None] * 2 + jnp.arange(2, dtype=jnp.int32)[None, :]
        par_slots = parents[:, None] * 2 + jnp.arange(2, dtype=jnp.int32)[None, :]
        codes = jnp.concatenate([place(two_slots, -1), place(par_slots, 1)], axis=1)
        scalars = jnp.concatenate([h_in[None], codes.reshape(8)]).astype(jnp.int32)
        return product_two(scalars, 2, g_hi, g_lo, gathered)

    pair_now = (z + 4) // 2
    h_next, part_one = lax.optimization_barrier((h_now, part_one[0, :8]))
    early = level_two(pair_now, h_next)
    h_last, early = lax.optimization_barrier((h_next, early))
    late = level_two(pair_now + 2, h_last)
    even = z % 2 == 0

    def term(d):
        take = lambda i: early[i] if i < 4 else late[i - 4]
        return jnp.where(even, take((d - 4) % 8), take((d - 3) % 8))

    up, down = term(4), term(-3)
    for d in range(3):
        up = lax.ppermute(up, "z", ring(8, 1)) + term(3 - d)
        down = lax.ppermute(down, "z", ring(8, -1))
        if d < 2:
            down = down + term(d - 2)
    inv_two = lax.ppermute(up, "z", ring(8, 1)) + down + term(0)
    panel_one = jnp.where(keep_one, inv_one.reshape(2, 256, 128), 0.0)
    panel_two = jnp.where(keep_two, inv_two.reshape(2, 256, 128), 0.0)

    dot_t = lambda a, b: lax.dot_general(a, b, (((0,), (0,)), ((), ())), precision=exact)
    lp_halves = []
    for t in range(2):
        code = place(mine * 2 + t, -1)
        at = (0, code // 8, h, code % 4, 1024, 0)
        lp_halves.append(lax.dynamic_slice(gathered, at, (2, 1, 1, 1, 128, 128)).reshape(256, 128))
    lp_own = jnp.concatenate(lp_halves, axis=1)
    scaled = jnp.dot(par[512:], lp_two, precision=exact)
    lp_slab = lax.dynamic_slice_in_dim(lp_own, row * 16, 16, 0)
    quad = dot_t(lp_slab, scaled)
    term_one = dot_t(own_one, inv_one)
    term_par = dot_t(par[:512], inv_two)
    term_two = quad - dot_t(own_two, inv_two) + dot_t(lp_own, term_par)
    terms = jnp.stack([term_one, term_par, term_two]).reshape(3, 16, 16, 128).transpose(1, 0, 2, 3)
    sums = jnp.sum(lax.all_to_all(terms, ROW_AXES, 0, 0), axis=0)
    diag_one = dinv_one - sums[0]
    parent_rows = -(sums[1] + scaled)
    diag_two = dinv_two + sums[2]
    return (panel_one, diag_one, panel_two, parent_rows, diag_two)


def solution(mesh):
    fine = jax.sharding.Mesh(mesh.devices.reshape(4, 2, 2, 2, 8), ALL_AXES)
    tall = P(None, ROW_AXES, COL_AXES)
    flat = P(ROW_AXES, COL_AXES)
    return jax.shard_map(
        local,
        mesh=fine,
        in_specs=(
            P(None, ROW_AXES, None, COL_AXES),
            tall,
            P(),
            flat,
            tall,
            P(None, COL_AXES),
            P(),
            P(),
            flat,
        ),
        out_specs=(tall, flat, tall, flat, flat),
        check_vma=False,
    )
```

```python
import functools

import jax
import jax.numpy as jnp
from jax import lax
from jax.experimental import pallas as pl
from jax.experimental.pallas import tpu as pltpu
from jax.sharding import PartitionSpec as P

ROW_AXES = ("x", "y_lo", "core")
COL_AXES = ("y_hi", "z")
ALL_AXES = ROW_AXES + COL_AXES
exact = lax.Precision.HIGHEST


def split(a):
    hi = a.astype(jnp.bfloat16)
    return hi, (a - hi.astype(jnp.float32)).astype(jnp.bfloat16)


def dot3(a, b):
    f = functools.partial(jnp.dot, preferred_element_type=jnp.float32)
    return f(a[0], b[0]) + (f(a[0], b[1]) + f(a[1], b[0]))


def one_kernel(sc_ref, gh_ref, gl_ref, a_ref, b_ref, out_ref):
    h = sc_ref[0]
    acc = None
    for k in range(2):
        half = h if k == 0 else 1 - h
        one = jnp.concatenate([a_ref[half, 0, 0, 0], b_ref[half, 0, 0, 0]], axis=1)
        term = dot3((gh_ref[k], gl_ref[k]), split(one))
        acc = term if acc is None else acc + term
    out_ref[0] = -acc[:, :128]
    out_ref[1] = -acc[:, 128:]


def two_kernel(sc_ref, gh_ref, gl_ref, *refs):
    twos, lps, pars, out_ref = refs[:4], refs[4:8], refs[8:10], refs[10]
    h = sc_ref[0]
    lp = jnp.concatenate(
        [jnp.concatenate([r[0, 0, 0] for r in lps[2 * t : 2 * t + 2]], axis=0) for t in range(2)],
        axis=1,
    )
    lp = split(lp)
    acc = None
    for k in range(2):
        half = h if k == 0 else 1 - h
        two = jnp.concatenate([twos[k][0, 0, 0], twos[2 + k][0, 0, 0]], axis=1)
        par = jnp.concatenate([r[half, 0, 0, 0] for r in pars], axis=1)
        folded = two - dot3(split(par), lp)
        term = dot3((gh_ref[k], gl_ref[k]), split(folded))
        acc = term if acc is None else acc + term
    out_ref[0] = -acc[:, :128]
    out_ref[1] = -acc[:, 128:]


WHOLE_G = pl.BlockSpec((2, 512, 512), lambda i, sc: (0, 0, 0))
PARAMS = pltpu.CompilerParams(vmem_limit_bytes=56 * 2**20)


def one_piece(first, stride):
    def place(i, sc):
        code = sc[first + stride * i]
        return (0, code // 8, code // 4 % 2, code % 4, 0, 0)

    return pl.BlockSpec((2, 1, 1, 1, 512, 128), place)


def two_piece(rows, block, first, stride):
    def place(i, sc):
        code = sc[first + stride * i]
        return (code // 8, code // 2 % 4, code % 2, block, 0)

    return pl.BlockSpec((1, 1, 1, rows, 128), place)


def product(kernel, pieces, flops, scalars, pairs, g_hi, g_lo, *gathered):
    return pl.pallas_call(
        kernel,
        grid_spec=pltpu.PrefetchScalarGridSpec(
            num_scalar_prefetch=1,
            grid=(pairs,),
            in_specs=[WHOLE_G, WHOLE_G, *pieces],
            out_specs=pl.BlockSpec((2, 512, 128), lambda i, sc: (i, 0, 0)),
        ),
        out_shape=jax.ShapeDtypeStruct((2 * pairs, 512, 128), jnp.float32),
        compiler_params=PARAMS,
        cost_estimate=pl.CostEstimate(
            flops=pairs * flops, bytes_accessed=pairs * 4_000_000, transcendentals=0
        ),
    )(scalars, g_hi, g_lo, *gathered)


ONE_PIECES = [one_piece(1 + t, 2) for t in range(2)]
TWO_PIECES = (
    [two_piece(512, 0, 1 + i, 10) for i in range(4)]
    + [two_piece(128, 4, 5 + i, 10) for i in range(4)]
    + [one_piece(9 + t, 10) for t in range(2)]
)


def chip_and_core(shift):
    up = (shift >= 1) & (shift <= 4)
    return (up * (4 - shift) + (1 - up) * (8 - shift)) % 4, 1 - up


def spread_pairs(sign):
    pairs = []
    for i in range(256):
        row, col = divmod(i, 16)
        half, z, h, s = row // 8, row % 8, col // 8, col % 8
        chip, core = chip_and_core(sign * (z - s) % 8)
        pairs.append((i, (half * 8 + chip * 2 + int(core)) * 16 + h * 8 + z))
    return pairs


def ring(n, step):
    return [(i, (i + step) % n) for i in range(n)]


def local(g_top, l_one, struct_one, dinv_one, l_two, lp_two, parent_two, pos_two, dinv_two):
    row = lax.axis_index(ROW_AXES)
    h = lax.axis_index("y_hi")
    z = lax.axis_index("z")
    mine = h * 4 + z // 2
    parent = parent_two[mine]

    blocks = jnp.arange(2, dtype=jnp.int32) * 16 + row
    list_one = lax.dynamic_index_in_dim(struct_one, mine, 0, keepdims=False)
    list_parent = lax.dynamic_index_in_dim(struct_one, parent, 0, keepdims=False)
    places = lax.dynamic_index_in_dim(pos_two, mine, 0, keepdims=False)
    picked = jnp.any(places[:, None] == jnp.arange(16)[None, :], axis=0)
    keep_one = jnp.any(list_one[None, :] == blocks[:, None], axis=1)[:, None, None]
    keep_two = jnp.any((list_parent[None, :] == blocks[:, None]) & picked[None, :], axis=1)
    keep_two = keep_two[:, None, None]
    one = jnp.where(keep_one, l_one, 0.0).reshape(512, 128)
    two = jnp.where(keep_two, l_two, 0.0).reshape(512, 128)

    lp_piece = lax.dynamic_slice_in_dim(lp_two, row // 8 * 128, 128, 0)
    near_one = lax.ppermute(one, ALL_AXES, spread_pairs(1))
    near_two = lax.ppermute(jnp.concatenate([two, lp_piece]), ALL_AXES, spread_pairs(-1))
    g_other = lax.ppermute(g_top, "y_hi", ring(2, 1))
    gathered = lax.all_gather(near_one, ("x", "y_hi", "y_lo", "core"), axis=0, tiled=False)
    gathered = gathered.reshape(2, 2, 2, 4, 512, 128)
    near_two, packed, two_sent, g_other = lax.optimization_barrier(
        (near_two, jnp.concatenate([one, dinv_one]), jnp.concatenate([two, lp_two]), g_other)
    )
    y_pair = jnp.stack([near_two, lax.ppermute(near_two, "y_lo", ring(2, 1))])
    x_all = jnp.stack([y_pair] + [lax.ppermute(y_pair, "x", ring(4, d)) for d in (1, 2, 3)])
    gathered_two = jnp.stack([x_all, lax.ppermute(x_all, "core", ring(2, 1))])

    def place_one(slot):
        chip, core = chip_and_core((z - slot) % 8)
        return chip // 2 * 8 + slot // 8 * 4 + chip % 2 * 2 + core

    def place_two(slot, half):
        chip, core = chip_and_core((slot - z) % 8)
        x_off = (lax.axis_index("x") - half * 2 - chip // 2) % 4
        y_off = lax.axis_index("y_lo") ^ (chip % 2)
        return (lax.axis_index("core") ^ core) * 8 + x_off * 2 + y_off

    g = jnp.stack([g_top, g_other]).reshape(2, 512, 512)
    g_hi32 = lax.reduce_precision(g, 8, 7)
    g_hi = g_hi32.astype(jnp.bfloat16)
    g_lo = (g - g_hi32).astype(jnp.bfloat16)

    pieces = {0: packed}
    right = left = packed
    for d in range(1, 5):
        right = lax.ppermute(right, "z", ring(8, 1))
        pieces[-d] = right
        if d < 4:
            left = lax.ppermute(left, "z", ring(8, -1))
            pieces[d] = left

    def fetch(super_index):
        parts = []
        for part in range(2):
            want = super_index % 4 * 2 + part
            total = jnp.zeros((528, 128), jnp.float32)
            for d, one_piece_here in pieces.items():
                total = jnp.where(want == (z + d) % 8, one_piece_here, total)
            parts.append(total)
        return jnp.concatenate(parts, axis=1)

    par_here = fetch(parent)
    par_there = fetch(parent_two[(1 - h) * 4 + z // 2])
    even = z % 2 == 0
    pair_up = lambda a, b: jnp.where(even, jnp.concatenate([a, b], 1), jnp.concatenate([b, a], 1))
    own_one = pair_up(one, jnp.where(even, pieces[1], pieces[-1])[:512])
    two_next = lax.ppermute(two_sent, "z", [(i, i ^ 1) for i in range(8)])
    own_two = pair_up(two, two_next[:512])
    lp_own = pair_up(lp_two, two_next[512:])

    slots = h * 8 + jnp.arange(8, dtype=jnp.int32)
    h_now, par_here, par_there, own_one, own_two, lp_own = lax.optimization_barrier(
        (h, par_here, par_there, own_one, own_two, lp_own)
    )
    scalars = jnp.concatenate([h_now[None], place_one(slots)]).astype(jnp.int32)
    part_one = product(
        one_kernel, ONE_PIECES, 800_000_000, scalars, 4, g_hi, g_lo, gathered, gathered
    )
    inv_one = lax.psum_scatter(part_one, "z", scatter_dimension=0, tiled=False)

    def level_two(first_pair, h_in):
        both = jnp.arange(2, dtype=jnp.int32)
        supers = h * 4 + (first_pair + both) % 4
        parents = parent_two.at[supers].get(mode="promise_in_bounds")
        two_slots = supers[:, None, None] * 2 + both[None, :, None]
        near_first = place_two(two_slots, jnp.where(both == 0, h, 1 - h)[None, None, :])
        in_order = place_two(two_slots, both[None, None, :])
        par_codes = place_one(parents[:, None] * 2 + both[None, :])
        codes = jnp.concatenate(
            [near_first.reshape(2, 4), in_order.reshape(2, 4), par_codes], axis=1
        )
        scalars = jnp.concatenate([h_in[None], codes.reshape(20)]).astype(jnp.int32)
        arrays = [gathered_two] * 8 + [gathered] * 2
        return product(two_kernel, TWO_PIECES, 1_600_000_000, scalars, 2, g_hi, g_lo, *arrays)

    pair_now = (z + 4) // 2
    h_next, part_one = lax.optimization_barrier((h_now, part_one[0, :8]))
    early = level_two(pair_now, h_next)
    h_last, early = lax.optimization_barrier((h_next, early))
    late = level_two(pair_now + 2, h_last)

    def term(d):
        take = lambda i: early[i] if i < 4 else late[i - 4]
        return jnp.where(even, take((d - 4) % 8), take((d - 3) % 8))

    up = lax.ppermute(term(4), "z", ring(8, 1))
    down = lax.ppermute(term(-3), "z", ring(8, -1))
    up, down, late = lax.optimization_barrier((up, down, late))
    up = lax.ppermute(up + term(3), "z", ring(8, 1))
    down = lax.ppermute(down + term(-2), "z", ring(8, -1))
    up = lax.ppermute(up + term(2), "z", ring(8, 1))
    down = lax.ppermute(down + term(-1), "z", ring(8, -1))
    inv_two = lax.ppermute(up + term(1), "z", ring(8, 1)) + down + term(0)
    par_other = lax.ppermute(par_there, "y_hi", ring(2, 1))
    par = jnp.where(parent // 4 == h, par_here, par_other)
    panel_one = jnp.where(keep_one, inv_one.reshape(2, 256, 128), 0.0)
    panel_two = jnp.where(keep_two, inv_two.reshape(2, 256, 128), 0.0)

    dot_t = lambda a, b: lax.dot_general(a, b, (((0,), (0,)), ((), ())), precision=exact)
    scaled = jnp.dot(par[512:], lp_two, precision=exact)
    lp_slab = lax.dynamic_slice_in_dim(lp_own, row * 16, 16, 0)
    quad = dot_t(lp_slab, scaled)
    term_one = dot_t(own_one, inv_one)
    term_par = dot_t(par[:512], inv_two)
    term_two = quad - dot_t(own_two, inv_two) + dot_t(lp_own, term_par)
    terms = jnp.stack([term_one, term_par, term_two]).reshape(3, 16, 16, 128).transpose(1, 0, 2, 3)
    sums = jnp.sum(lax.all_to_all(terms, ROW_AXES, 0, 0), axis=0)
    diag_one = dinv_one - sums[0]
    parent_rows = -(sums[1] + scaled)
    diag_two = dinv_two + sums[2]
    return (panel_one, diag_one, panel_two, parent_rows, diag_two)


def solution(mesh):
    fine = jax.sharding.Mesh(mesh.devices.reshape(4, 2, 2, 2, 8), ALL_AXES)
    tall = P(None, ROW_AXES, COL_AXES)
    flat = P(ROW_AXES, COL_AXES)
    return jax.shard_map(
        local,
        mesh=fine,
        in_specs=(
            P(None, ROW_AXES, None, COL_AXES),
            tall,
            P(),
            flat,
            tall,
            P(None, COL_AXES),
            P(),
            P(),
            flat,
        ),
        out_specs=(tall, flat, tall, flat, flat),
        check_vma=False,
    )
```

```python
import functools

import jax
import jax.numpy as jnp
from jax import lax
from jax.experimental import pallas as pl
from jax.experimental.pallas import tpu as pltpu
from jax.sharding import PartitionSpec as P

ROW_AXES = ("x", "y_lo", "core")
COL_AXES = ("y_hi", "z")
ALL_AXES = ROW_AXES + COL_AXES
exact = lax.Precision.HIGHEST


def split(a):
    hi = a.astype(jnp.bfloat16)
    return hi, (a - hi.astype(jnp.float32)).astype(jnp.bfloat16)


def dot3(a, b):
    f = functools.partial(jnp.dot, preferred_element_type=jnp.float32)
    return f(a[0], b[0]) + (f(a[0], b[1]) + f(a[1], b[0]))


def pair_kernel(sc_ref, gh_ref, gl_ref, a_ref, b_ref, out_ref):
    h = sc_ref[0]
    acc = None
    for k in range(2):
        half = h if k == 0 else 1 - h
        cols = jnp.concatenate([a_ref[half, 0, 0], b_ref[half, 0, 0]], axis=1)
        term = dot3((gh_ref[k], gl_ref[k]), split(cols))
        acc = term if acc is None else acc + term
    out_ref[0] = -acc[:, :128]
    out_ref[1] = -acc[:, 128:]


WHOLE_G = pl.BlockSpec((2, 512, 512), lambda i, sc: (0, 0, 0))
PARAMS = pltpu.CompilerParams(vmem_limit_bytes=40 * 2**20)


def slot_rows(first):
    def place(i, sc):
        code = sc[first + 2 * i]
        return (0, code // 4, code % 4, 0, 0)

    return pl.BlockSpec((2, 1, 1, 512, 128), place)


def product(scalars, g_hi, g_lo, gathered):
    return pl.pallas_call(
        pair_kernel,
        grid_spec=pltpu.PrefetchScalarGridSpec(
            num_scalar_prefetch=1,
            grid=(2,),
            in_specs=[WHOLE_G, WHOLE_G, slot_rows(1), slot_rows(2)],
            out_specs=pl.BlockSpec((2, 512, 128), lambda i, sc: (i, 0, 0)),
        ),
        out_shape=jax.ShapeDtypeStruct((4, 512, 128), jnp.float32),
        compiler_params=PARAMS,
        cost_estimate=pl.CostEstimate(
            flops=1_600_000_000, bytes_accessed=7_000_000, transcendentals=0
        ),
    )(scalars, g_hi, g_lo, gathered, gathered)


def chip_and_core(shift):
    up = (shift >= 1) & (shift <= 4)
    return (up * (4 - shift) + (1 - up) * (8 - shift)) % 4, 1 - up


def spread_pairs():
    pairs = []
    for i in range(256):
        row, col = divmod(i, 16)
        half, z, h, s = row // 8, row % 8, col // 8, col % 8
        chip, core = chip_and_core((z - s) % 8)
        pairs.append((i, (half * 8 + chip * 2 + int(core)) * 16 + h * 8 + z))
    return pairs


def ring(n, step):
    return [(i, (i + step) % n) for i in range(n)]


def local(g_top, l_one, struct_one, dinv_one, l_two, lp_two, parent_two, pos_two, dinv_two):
    row = lax.axis_index(ROW_AXES)
    h = lax.axis_index("y_hi")
    z = lax.axis_index("z")
    mine = h * 4 + z // 2
    parent = parent_two[mine]

    blocks = jnp.arange(2, dtype=jnp.int32) * 16 + row
    list_one = lax.dynamic_index_in_dim(struct_one, mine, 0, keepdims=False)
    list_parent = lax.dynamic_index_in_dim(struct_one, parent, 0, keepdims=False)
    places = lax.dynamic_index_in_dim(pos_two, mine, 0, keepdims=False)
    picked = jnp.any(places[:, None] == jnp.arange(16)[None, :], axis=0)
    keep_one = jnp.any(list_one[None, :] == blocks[:, None], axis=1)[:, None, None]
    keep_two = jnp.any((list_parent[None, :] == blocks[:, None]) & picked[None, :], axis=1)
    keep_two = keep_two[:, None, None]
    one = jnp.where(keep_one, l_one, 0.0).reshape(512, 128)
    two = jnp.where(keep_two, l_two, 0.0).reshape(512, 128)

    def gather(piece):
        rows = lax.all_gather(piece, ROW_AXES, axis=0, tiled=False)
        return rows.reshape(2, 2, 4, 512, 128)

    g_other = lax.ppermute(g_top, "y_hi", ring(2, 1))
    packed = jnp.concatenate([one, dinv_one])
    pieces = {0: packed}
    right = left = packed
    sent = one
    for d in range(1, 5):
        right = lax.ppermute(right, "z", ring(8, 1))
        if d < 4:
            left = lax.ppermute(left, "z", ring(8, -1))
        if d == 1:
            right, left, sent = lax.optimization_barrier((right, left, sent))
            near_one = lax.ppermute(sent, ALL_AXES, spread_pairs())
        if d == 4:
            right, left, near_one, g_other = lax.optimization_barrier(
                (right, left, near_one, g_other)
            )
        pieces[-d] = right
        if d < 4:
            pieces[d] = left
    gathered_one = gather(near_one)

    g = jnp.stack([g_top, g_other]).reshape(2, 512, 512)
    g_hi32 = lax.reduce_precision(g, 8, 7)
    g_hi = g_hi32.astype(jnp.bfloat16)
    g_lo = (g - g_hi32).astype(jnp.bfloat16)

    def fetch(super_index):
        parts = []
        for part in range(2):
            want = super_index % 4 * 2 + part
            total = jnp.zeros((528, 128), jnp.float32)
            for d, one_piece_here in pieces.items():
                total = jnp.where(want == (z + d) % 8, one_piece_here, total)
            parts.append(total)
        return jnp.concatenate(parts, axis=1)

    par_here = fetch(parent)
    par_there = fetch(parent_two[(1 - h) * 4 + z // 2])
    even = z % 2 == 0
    pair_up = lambda a, b: jnp.where(even, jnp.concatenate([a, b], 1), jnp.concatenate([b, a], 1))
    own_one = pair_up(one, jnp.where(even, pieces[1], pieces[-1])[:512])
    par_other = lax.ppermute(par_there, "y_hi", ring(2, 1))
    par = jnp.where(parent // 4 == h, par_here, par_other)
    folded = two - jnp.dot(par[:512], lp_two, precision=lax.Precision.HIGH)
    gathered_two = gather(lax.ppermute(folded, ALL_AXES, spread_pairs()))
    two_sent = jnp.concatenate([two, lp_two])
    two_next = lax.ppermute(two_sent, "z", [(i, i ^ 1) for i in range(8)])
    own_two = pair_up(two, two_next[:512])
    lp_own = pair_up(lp_two, two_next[512:])

    def multiply_and_sum(gathered, after):
        def part(first_pair, after):
            both = jnp.arange(2, dtype=jnp.int32)
            slots = (first_pair + both) % 4 * 2
            chip, core = chip_and_core((z - slots[:, None] - both[None, :]) % 8)
            codes = chip // 2 * 4 + chip % 2 * 2 + core
            scalars = jnp.concatenate([after[None], codes.reshape(4)]).astype(jnp.int32)
            return product(scalars, g_hi, g_lo, gathered)

        early = part((z + 4) // 2, after)
        after, early = lax.optimization_barrier((after, early))
        late = part((z + 4) // 2 + 2, after)

        def term(d):
            take = lambda i: early[i] if i < 4 else late[i - 4]
            return jnp.where(even, take((d - 4) % 8), take((d - 3) % 8))

        up = lax.ppermute(term(4), "z", ring(8, 1))
        down = lax.ppermute(term(-3), "z", ring(8, -1))
        up, down, late = lax.optimization_barrier((up, down, late))
        up = lax.ppermute(up + term(3), "z", ring(8, 1))
        down = lax.ppermute(down + term(-2), "z", ring(8, -1))
        up = lax.ppermute(up + term(2), "z", ring(8, 1))
        down = lax.ppermute(down + term(-1), "z", ring(8, -1))
        return lax.ppermute(up + term(1), "z", ring(8, 1)) + down + term(0)

    inv_one = multiply_and_sum(gathered_one, h)
    inv_one, own_one, own_two, lp_own, h_next = lax.optimization_barrier(
        (inv_one, own_one, own_two, lp_own, h)
    )
    inv_two = multiply_and_sum(gathered_two, h_next)
    panel_one = jnp.where(keep_one, inv_one.reshape(2, 256, 128), 0.0)
    panel_two = jnp.where(keep_two, inv_two.reshape(2, 256, 128), 0.0)

    dot_t = lambda a, b: lax.dot_general(a, b, (((0,), (0,)), ((), ())), precision=exact)
    scaled = jnp.dot(par[512:], lp_two, precision=exact)
    lp_slab = lax.dynamic_slice_in_dim(lp_own, row * 16, 16, 0)
    quad = dot_t(lp_slab, scaled)
    term_one = dot_t(own_one, inv_one)
    term_par = dot_t(par[:512], inv_two)
    term_two = quad - dot_t(own_two, inv_two) + dot_t(lp_own, term_par)
    terms = jnp.stack([term_one, term_par, term_two]).reshape(3, 16, 16, 128).transpose(1, 0, 2, 3)
    sums = jnp.sum(lax.all_to_all(terms, ROW_AXES, 0, 0), axis=0)
    diag_one = dinv_one - sums[0]
    parent_rows = -(sums[1] + scaled)
    diag_two = dinv_two + sums[2]
    return (panel_one, diag_one, panel_two, parent_rows, diag_two)


def solution(mesh):
    fine = jax.sharding.Mesh(mesh.devices.reshape(4, 2, 2, 2, 8), ALL_AXES)
    tall = P(None, ROW_AXES, COL_AXES)
    flat = P(ROW_AXES, COL_AXES)
    return jax.shard_map(
        local,
        mesh=fine,
        in_specs=(
            P(None, ROW_AXES, None, COL_AXES),
            tall,
            P(),
            flat,
            tall,
            P(None, COL_AXES),
            P(),
            P(),
            flat,
        ),
        out_specs=(tall, flat, tall, flat, flat),
        check_vma=False,
    )
```

```python
import functools

import jax
import jax.numpy as jnp
from jax import lax
from jax.experimental import pallas as pl
from jax.experimental.pallas import tpu as pltpu
from jax.sharding import PartitionSpec as P

ROW_AXES = ("x", "y_lo", "core")
COL_AXES = ("y_hi", "z")
ALL_AXES = ROW_AXES + COL_AXES
exact = lax.Precision.HIGHEST


def split(a):
    hi = a.astype(jnp.bfloat16)
    return hi, (a - hi.astype(jnp.float32)).astype(jnp.bfloat16)


def dot3(a, b):
    f = functools.partial(jnp.dot, preferred_element_type=jnp.float32)
    return f(a[0], b[0]) + (f(a[0], b[1]) + f(a[1], b[0]))


def pair_kernel(sc_ref, gh_ref, gl_ref, a_ref, b_ref, out_ref):
    h = sc_ref[0]
    acc = None
    for k in range(2):
        half = h if k == 0 else 1 - h
        cols = jnp.concatenate([a_ref[half, 0, 0], b_ref[half, 0, 0]], axis=1)
        term = dot3((gh_ref[k], gl_ref[k]), split(cols))
        acc = term if acc is None else acc + term
    out_ref[0] = -acc[:, :128]
    out_ref[1] = -acc[:, 128:]


WHOLE_G = pl.BlockSpec((2, 512, 512), lambda i, sc: (0, 0, 0))
PARAMS = pltpu.CompilerParams(vmem_limit_bytes=40 * 2**20)


def slot_rows(first):
    def place(i, sc):
        code = sc[first + 2 * i]
        return (0, code // 4, code % 4, 0, 0)

    return pl.BlockSpec((2, 1, 1, 512, 128), place)


def product(scalars, g_hi, g_lo, gathered):
    return pl.pallas_call(
        pair_kernel,
        grid_spec=pltpu.PrefetchScalarGridSpec(
            num_scalar_prefetch=1,
            grid=(2,),
            in_specs=[WHOLE_G, WHOLE_G, slot_rows(1), slot_rows(2)],
            out_specs=pl.BlockSpec((2, 512, 128), lambda i, sc: (i, 0, 0)),
        ),
        out_shape=jax.ShapeDtypeStruct((4, 512, 128), jnp.float32),
        compiler_params=PARAMS,
        cost_estimate=pl.CostEstimate(
            flops=1_600_000_000, bytes_accessed=7_000_000, transcendentals=0
        ),
    )(scalars, g_hi, g_lo, gathered, gathered)


def chip_and_core(shift):
    up = (shift >= 1) & (shift <= 4)
    return (up * (4 - shift) + (1 - up) * (8 - shift)) % 4, 1 - up


def spread_pairs():
    pairs = []
    for i in range(256):
        row, col = divmod(i, 16)
        half, z, h, s = row // 8, row % 8, col // 8, col % 8
        chip, core = chip_and_core((z - s) % 8)
        pairs.append((i, (half * 8 + chip * 2 + int(core)) * 16 + h * 8 + z))
    return pairs


def ring(n, step):
    return [(i, (i + step) % n) for i in range(n)]


def local(g_top, l_one, struct_one, dinv_one, l_two, lp_two, parent_two, pos_two, dinv_two):
    row = lax.axis_index(ROW_AXES)
    h = lax.axis_index("y_hi")
    z = lax.axis_index("z")
    mine = h * 4 + z // 2
    parent = parent_two[mine]

    blocks = jnp.arange(2, dtype=jnp.int32) * 16 + row
    list_one = lax.dynamic_index_in_dim(struct_one, mine, 0, keepdims=False)
    list_parent = lax.dynamic_index_in_dim(struct_one, parent, 0, keepdims=False)
    places = lax.dynamic_index_in_dim(pos_two, mine, 0, keepdims=False)
    picked = jnp.any(places[:, None] == jnp.arange(16)[None, :], axis=0)
    keep_one = jnp.any(list_one[None, :] == blocks[:, None], axis=1)[:, None, None]
    keep_two = jnp.any((list_parent[None, :] == blocks[:, None]) & picked[None, :], axis=1)
    keep_two = keep_two[:, None, None]
    one = jnp.where(keep_one, l_one, 0.0).reshape(512, 128)
    two = jnp.where(keep_two, l_two, 0.0).reshape(512, 128)

    def gather(piece):
        rows = lax.all_gather(piece, ROW_AXES, axis=0, tiled=False)
        return rows.reshape(2, 2, 4, 512, 128)

    g_other = lax.ppermute(g_top, "y_hi", ring(2, 1))
    near_one = lax.ppermute(one, ALL_AXES, spread_pairs())
    packed = jnp.concatenate([one, dinv_one])
    pieces = {0: packed}
    right = left = packed
    for d in range(1, 5):
        right = lax.ppermute(right, "z", ring(8, 1))
        if d < 4:
            left = lax.ppermute(left, "z", ring(8, -1))
            if d == 1:
                right, left, near_one, g_other = lax.optimization_barrier(
                    (right, left, near_one, g_other)
                )
            pieces[d] = left
        pieces[-d] = right
    gathered_one = gather(near_one)

    g = jnp.stack([g_top, g_other]).reshape(2, 512, 512)
    g_hi32 = lax.reduce_precision(g, 8, 7)
    g_hi = g_hi32.astype(jnp.bfloat16)
    g_lo = (g - g_hi32).astype(jnp.bfloat16)

    def fetch(super_index):
        parts = []
        for part in range(2):
            want = super_index % 4 * 2 + part
            total = jnp.zeros((528, 128), jnp.float32)
            for d, one_piece_here in pieces.items():
                total = jnp.where(want == (z + d) % 8, one_piece_here, total)
            parts.append(total)
        return jnp.concatenate(parts, axis=1)

    par_here = fetch(parent)
    par_there = fetch(parent_two[(1 - h) * 4 + z // 2])
    even = z % 2 == 0
    pair_up = lambda a, b: jnp.where(even, jnp.concatenate([a, b], 1), jnp.concatenate([b, a], 1))
    own_one = pair_up(one, jnp.where(even, pieces[1], pieces[-1])[:512])
    par_other = lax.ppermute(par_there, "y_hi", ring(2, 1))
    par = jnp.where(parent // 4 == h, par_here, par_other)
    folded = two - jnp.dot(par[:512], lp_two, precision=lax.Precision.HIGH)
    gathered_two = gather(lax.ppermute(folded, ALL_AXES, spread_pairs()))
    two_sent = jnp.concatenate([two, lp_two])
    two_next = lax.ppermute(two_sent, "z", [(i, i ^ 1) for i in range(8)])
    own_two = pair_up(two, two_next[:512])
    lp_own = pair_up(lp_two, two_next[512:])

    def multiply_and_sum(gathered, after):
        def part(first_pair, after):
            both = jnp.arange(2, dtype=jnp.int32)
            slots = (first_pair + both) % 4 * 2
            chip, core = chip_and_core((z - slots[:, None] - both[None, :]) % 8)
            codes = chip // 2 * 4 + chip % 2 * 2 + core
            scalars = jnp.concatenate([after[None], codes.reshape(4)]).astype(jnp.int32)
            return product(scalars, g_hi, g_lo, gathered)

        early = part((z + 4) // 2, after)
        after, early = lax.optimization_barrier((after, early))
        late = part((z + 4) // 2 + 2, after)

        def term(d):
            take = lambda i: early[i] if i < 4 else late[i - 4]
            return jnp.where(even, take((d - 4) % 8), take((d - 3) % 8))

        up = lax.ppermute(term(4), "z", ring(8, 1))
        down = lax.ppermute(term(-3), "z", ring(8, -1))
        up, down, late = lax.optimization_barrier((up, down, late))
        up = lax.ppermute(up + term(3), "z", ring(8, 1))
        down = lax.ppermute(down + term(-2), "z", ring(8, -1))
        up = lax.ppermute(up + term(2), "z", ring(8, 1))
        down = lax.ppermute(down + term(-1), "z", ring(8, -1))
        return lax.ppermute(up + term(1), "z", ring(8, 1)) + down + term(0)

    inv_one = multiply_and_sum(gathered_one, h)
    inv_one, own_one, own_two, lp_own, h_next = lax.optimization_barrier(
        (inv_one, own_one, own_two, lp_own, h)
    )
    inv_two = multiply_and_sum(gathered_two, h_next)
    panel_one = jnp.where(keep_one, inv_one.reshape(2, 256, 128), 0.0)
    panel_two = jnp.where(keep_two, inv_two.reshape(2, 256, 128), 0.0)

    dot_t = lambda a, b: lax.dot_general(a, b, (((0,), (0,)), ((), ())), precision=exact)
    scaled = jnp.dot(par[512:], lp_two, precision=exact)
    lp_slab = lax.dynamic_slice_in_dim(lp_own, row * 16, 16, 0)
    quad = dot_t(lp_slab, scaled)
    term_one = dot_t(own_one, inv_one)
    term_par = dot_t(par[:512], inv_two)
    term_two = quad - dot_t(own_two, inv_two) + dot_t(lp_own, term_par)
    terms = jnp.stack([term_one, term_par, term_two]).reshape(3, 16, 16, 128).transpose(1, 0, 2, 3)
    sums = jnp.sum(lax.all_to_all(terms, ROW_AXES, 0, 0), axis=0)
    diag_one = dinv_one - sums[0]
    parent_rows = -(sums[1] + scaled)
    diag_two = dinv_two + sums[2]
    return (panel_one, diag_one, panel_two, parent_rows, diag_two)


def solution(mesh):
    fine = jax.sharding.Mesh(mesh.devices.reshape(4, 2, 2, 2, 8), ALL_AXES)
    tall = P(None, ROW_AXES, COL_AXES)
    flat = P(ROW_AXES, COL_AXES)
    return jax.shard_map(
        local,
        mesh=fine,
        in_specs=(
            P(None, ROW_AXES, None, COL_AXES),
            tall,
            P(),
            flat,
            tall,
            P(None, COL_AXES),
            P(),
            P(),
            flat,
        ),
        out_specs=(tall, flat, tall, flat, flat),
        check_vma=False,
    )
```

```python
import functools

import jax
import jax.numpy as jnp
from jax import lax
from jax.experimental import pallas as pl
from jax.experimental.pallas import tpu as pltpu
from jax.sharding import PartitionSpec as P

ROW_AXES = ("x", "y_lo", "core")
COL_AXES = ("y_hi", "z")
ALL_AXES = ROW_AXES + COL_AXES
exact = lax.Precision.HIGHEST


def split(a):
    hi = a.astype(jnp.bfloat16)
    return hi, (a - hi.astype(jnp.float32)).astype(jnp.bfloat16)


def dot3(a, b):
    f = functools.partial(jnp.dot, preferred_element_type=jnp.float32)
    return f(a[0], b[0]) + (f(a[0], b[1]) + f(a[1], b[0]))


def pair_kernel(sc_ref, gh_ref, gl_ref, a_ref, b_ref, out_ref):
    h = sc_ref[0]
    acc = None
    for k in range(2):
        half = h if k == 0 else 1 - h
        cols = jnp.concatenate([a_ref[half, 0, 0], b_ref[half, 0, 0]], axis=1)
        term = dot3((gh_ref[k], gl_ref[k]), split(cols))
        acc = term if acc is None else acc + term
    out_ref[0] = -acc[:, :128]
    out_ref[1] = -acc[:, 128:]


WHOLE_G = pl.BlockSpec((2, 512, 512), lambda i, sc: (0, 0, 0))
PARAMS = pltpu.CompilerParams(vmem_limit_bytes=40 * 2**20)


def slot_rows(first):
    def place(i, sc):
        code = sc[first + 2 * i]
        return (0, code // 4, code % 4, 0, 0)

    return pl.BlockSpec((2, 1, 1, 512, 128), place)


def product(scalars, g_hi, g_lo, gathered):
    return pl.pallas_call(
        pair_kernel,
        grid_spec=pltpu.PrefetchScalarGridSpec(
            num_scalar_prefetch=1,
            grid=(2,),
            in_specs=[WHOLE_G, WHOLE_G, slot_rows(1), slot_rows(2)],
            out_specs=pl.BlockSpec((2, 512, 128), lambda i, sc: (i, 0, 0)),
        ),
        out_shape=jax.ShapeDtypeStruct((4, 512, 128), jnp.float32),
        compiler_params=PARAMS,
        cost_estimate=pl.CostEstimate(
            flops=1_600_000_000, bytes_accessed=7_000_000, transcendentals=0
        ),
    )(scalars, g_hi, g_lo, gathered, gathered)


def chip_and_core(shift):
    up = (shift >= 1) & (shift <= 4)
    return (up * (4 - shift) + (1 - up) * (8 - shift)) % 4, 1 - up


def spread_pairs():
    pairs = []
    for i in range(256):
        row, col = divmod(i, 16)
        half, z, h, s = row // 8, row % 8, col // 8, col % 8
        chip, core = chip_and_core((z - s) % 8)
        pairs.append((i, (half * 8 + chip * 2 + int(core)) * 16 + h * 8 + z))
    return pairs


def ring(n, step):
    return [(i, (i + step) % n) for i in range(n)]


def local(g_top, l_one, struct_one, dinv_one, l_two, lp_two, parent_two, pos_two, dinv_two):
    row = lax.axis_index(ROW_AXES)
    h = lax.axis_index("y_hi")
    z = lax.axis_index("z")
    mine = h * 4 + z // 2
    parent = parent_two[mine]

    blocks = jnp.arange(2, dtype=jnp.int32) * 16 + row
    list_one = lax.dynamic_index_in_dim(struct_one, mine, 0, keepdims=False)
    list_parent = lax.dynamic_index_in_dim(struct_one, parent, 0, keepdims=False)
    places = lax.dynamic_index_in_dim(pos_two, mine, 0, keepdims=False)
    picked = jnp.any(places[:, None] == jnp.arange(16)[None, :], axis=0)
    keep_one = jnp.any(list_one[None, :] == blocks[:, None], axis=1)[:, None, None]
    keep_two = jnp.any((list_parent[None, :] == blocks[:, None]) & picked[None, :], axis=1)
    keep_two = keep_two[:, None, None]
    one = jnp.where(keep_one, l_one, 0.0).reshape(512, 128)
    two = jnp.where(keep_two, l_two, 0.0).reshape(512, 128)

    def gather(piece):
        rows = lax.all_gather(piece, ROW_AXES, axis=0, tiled=False)
        return rows.reshape(2, 2, 4, 512, 128)

    g_other = lax.ppermute(g_top, "y_hi", ring(2, 1))
    lp_far = lax.ppermute(lp_two, "y_hi", ring(2, 1))
    near_one = lax.ppermute(one, ALL_AXES, spread_pairs())
    packed = jnp.concatenate([one, dinv_one])
    pieces = {0: packed}
    right = left = packed
    for d in range(1, 5):
        right = lax.ppermute(right, "z", ring(8, 1))
        if d < 4:
            left = lax.ppermute(left, "z", ring(8, -1))
            if d == 1:
                right, left, near_one = lax.optimization_barrier((right, left, near_one))
            pieces[d] = left
        pieces[-d] = right
    pieces[-4], g_other, lp_far = lax.optimization_barrier((right, g_other, lp_far))
    gathered_one = gather(near_one)

    g = jnp.stack([g_top, g_other]).reshape(2, 512, 512)
    g_hi32 = lax.reduce_precision(g, 8, 7)
    g_hi = g_hi32.astype(jnp.bfloat16)
    g_lo = (g - g_hi32).astype(jnp.bfloat16)

    def fetch(super_index):
        parts = []
        for part in range(2):
            want = super_index % 4 * 2 + part
            total = jnp.zeros((528, 128), jnp.float32)
            for d, one_piece_here in pieces.items():
                total = jnp.where(want == (z + d) % 8, one_piece_here, total)
            parts.append(total)
        return jnp.concatenate(parts, axis=1)

    par_here = fetch(parent)
    par_there = fetch(parent_two[(1 - h) * 4 + z // 2])
    even = z % 2 == 0
    pair_up = lambda a, b: jnp.where(even, jnp.concatenate([a, b], 1), jnp.concatenate([b, a], 1))
    own_one = pair_up(one, jnp.where(even, pieces[1], pieces[-1])[:512])
    here = parent // 4 == h
    by_lp = lambda cols, lp: jnp.dot(cols[:512], lp, precision=lax.Precision.HIGH)
    from_far = lax.ppermute(by_lp(par_there, lp_far), "y_hi", ring(2, 1))
    folded = two - jnp.where(here, by_lp(par_here, lp_two), from_far)
    near_two = lax.ppermute(folded, ALL_AXES, spread_pairs())
    two_sent = jnp.concatenate([two, lp_two])
    two_next = lax.ppermute(two_sent, "z", [(i, i ^ 1) for i in range(8)])
    own_two = pair_up(two, two_next[:512])
    lp_own = pair_up(lp_two, two_next[512:])

    def multiply(gathered, after):
        def part(first_pair, after):
            both = jnp.arange(2, dtype=jnp.int32)
            slots = (first_pair + both) % 4 * 2
            chip, core = chip_and_core((z - slots[:, None] - both[None, :]) % 8)
            codes = chip // 2 * 4 + chip % 2 * 2 + core
            scalars = jnp.concatenate([after[None], codes.reshape(4)]).astype(jnp.int32)
            return product(scalars, g_hi, g_lo, gathered)

        early = part((z + 4) // 2, after)
        after, early = lax.optimization_barrier((after, early))
        return early, part((z + 4) // 2 + 2, after)

    def sum_over_z(early, late):
        def term(d):
            take = lambda i: early[i] if i < 4 else late[i - 4]
            return jnp.where(even, take((d - 4) % 8), take((d - 3) % 8))

        up = lax.ppermute(term(4), "z", ring(8, 1))
        down = lax.ppermute(term(-3), "z", ring(8, -1))
        up, down, late = lax.optimization_barrier((up, down, late))
        up = lax.ppermute(up + term(3), "z", ring(8, 1))
        down = lax.ppermute(down + term(-2), "z", ring(8, -1))
        up = lax.ppermute(up + term(2), "z", ring(8, 1))
        down = lax.ppermute(down + term(-1), "z", ring(8, -1))
        return lax.ppermute(up + term(1), "z", ring(8, 1)) + down + term(0)

    early, late = multiply(gathered_one, h)
    near_two, early, late = lax.optimization_barrier((near_two, early, late))
    gathered_two = gather(near_two)
    inv_one = sum_over_z(early, late)
    inv_one, own_one, own_two, lp_own, par_there, h_next = lax.optimization_barrier(
        (inv_one, own_one, own_two, lp_own, par_there, h)
    )
    par = jnp.where(here, par_here, lax.ppermute(par_there, "y_hi", ring(2, 1)))
    inv_two = sum_over_z(*multiply(gathered_two, h_next))
    panel_one = jnp.where(keep_one, inv_one.reshape(2, 256, 128), 0.0)
    panel_two = jnp.where(keep_two, inv_two.reshape(2, 256, 128), 0.0)

    dot_t = lambda a, b: lax.dot_general(a, b, (((0,), (0,)), ((), ())), precision=exact)
    scaled = jnp.dot(par[512:], lp_two, precision=exact)
    lp_slab = lax.dynamic_slice_in_dim(lp_own, row * 16, 16, 0)
    quad = dot_t(lp_slab, scaled)
    term_one = dot_t(own_one, inv_one)
    term_par = dot_t(par[:512], inv_two)
    term_two = quad - dot_t(own_two, inv_two) + dot_t(lp_own, term_par)
    terms = jnp.stack([term_one, term_par, term_two]).reshape(3, 16, 16, 128).transpose(1, 0, 2, 3)
    sums = jnp.sum(lax.all_to_all(terms, ROW_AXES, 0, 0), axis=0)
    diag_one = dinv_one - sums[0]
    parent_rows = -(sums[1] + scaled)
    diag_two = dinv_two + sums[2]
    return (panel_one, diag_one, panel_two, parent_rows, diag_two)


def solution(mesh):
    fine = jax.sharding.Mesh(mesh.devices.reshape(4, 2, 2, 2, 8), ALL_AXES)
    tall = P(None, ROW_AXES, COL_AXES)
    flat = P(ROW_AXES, COL_AXES)
    return jax.shard_map(
        local,
        mesh=fine,
        in_specs=(
            P(None, ROW_AXES, None, COL_AXES),
            tall,
            P(),
            flat,
            tall,
            P(None, COL_AXES),
            P(),
            P(),
            flat,
        ),
        out_specs=(tall, flat, tall, flat, flat),
        check_vma=False,
    )
```

```python
import functools

import jax
import jax.numpy as jnp
from jax import lax
from jax.experimental import pallas as pl
from jax.experimental.pallas import tpu as pltpu
from jax.sharding import PartitionSpec as P

ROW_AXES = ("x", "y_lo", "core")
COL_AXES = ("y_hi", "z")
ALL_AXES = ROW_AXES + COL_AXES
exact = lax.Precision.HIGHEST


def split(a):
    hi = a.astype(jnp.bfloat16)
    return hi, (a - hi.astype(jnp.float32)).astype(jnp.bfloat16)


def dot3(a, b):
    f = functools.partial(jnp.dot, preferred_element_type=jnp.float32)
    return f(a[0], b[0]) + (f(a[0], b[1]) + f(a[1], b[0]))


def pair_kernel(sc_ref, *refs):
    g_refs, (a_ref, b_ref, out_ref) = refs[:4], refs[4:]
    h = sc_ref[0]
    acc = None
    for k in range(2):
        half = h if k == 0 else 1 - h
        cols = jnp.concatenate([a_ref[half, 0, 0], b_ref[half, 0, 0]], axis=1)
        term = dot3((g_refs[2 * k][...], g_refs[2 * k + 1][...]), split(cols))
        acc = term if acc is None else acc + term
    out_ref[0] = -acc[:, :128]
    out_ref[1] = -acc[:, 128:]


WHOLE_G = pl.BlockSpec((512, 512), lambda i, sc: (0, 0))
PARAMS = pltpu.CompilerParams(vmem_limit_bytes=40 * 2**20)


def slot_rows(first):
    def place(i, sc):
        code = sc[first + 2 * i]
        return (0, code // 4, code % 4, 0, 0)

    return pl.BlockSpec((2, 1, 1, 512, 128), place)


def product(scalars, g_parts, gathered):
    return pl.pallas_call(
        pair_kernel,
        grid_spec=pltpu.PrefetchScalarGridSpec(
            num_scalar_prefetch=1,
            grid=(2,),
            in_specs=[WHOLE_G] * 4 + [slot_rows(1), slot_rows(2)],
            out_specs=pl.BlockSpec((2, 512, 128), lambda i, sc: (i, 0, 0)),
        ),
        out_shape=jax.ShapeDtypeStruct((4, 512, 128), jnp.float32),
        compiler_params=PARAMS,
        cost_estimate=pl.CostEstimate(
            flops=1_600_000_000, bytes_accessed=7_000_000, transcendentals=0
        ),
    )(scalars, *g_parts, gathered, gathered)


def chip_and_core(shift):
    up = (shift >= 1) & (shift <= 4)
    return (up * (4 - shift) + (1 - up) * (8 - shift)) % 4, 1 - up


def spread_pairs():
    pairs = []
    for i in range(256):
        row, col = divmod(i, 16)
        half, z, h, s = row // 8, row % 8, col // 8, col % 8
        chip, core = chip_and_core((z - s) % 8)
        pairs.append((i, (half * 8 + chip * 2 + int(core)) * 16 + h * 8 + z))
    return pairs


def ring(n, step):
    return [(i, (i + step) % n) for i in range(n)]


def local(g_top, l_one, struct_one, dinv_one, l_two, lp_two, parent_two, pos_two, dinv_two):
    row = lax.axis_index(ROW_AXES)
    h = lax.axis_index("y_hi")
    z = lax.axis_index("z")
    mine = h * 4 + z // 2
    parent = parent_two[mine]

    blocks = jnp.arange(2, dtype=jnp.int32) * 16 + row
    list_one = lax.dynamic_index_in_dim(struct_one, mine, 0, keepdims=False)
    list_parent = lax.dynamic_index_in_dim(struct_one, parent, 0, keepdims=False)
    places = lax.dynamic_index_in_dim(pos_two, mine, 0, keepdims=False)
    picked = jnp.any(places[:, None] == jnp.arange(16)[None, :], axis=0)
    keep_one = jnp.any(list_one[None, :] == blocks[:, None], axis=1)[:, None, None]
    keep_two = jnp.any((list_parent[None, :] == blocks[:, None]) & picked[None, :], axis=1)
    keep_two = keep_two[:, None, None]
    one = jnp.where(keep_one, l_one, 0.0).reshape(512, 128)
    two = jnp.where(keep_two, l_two, 0.0).reshape(512, 128)

    def gather(piece):
        rows = lax.all_gather(piece, ROW_AXES, axis=0, tiled=False)
        return rows.reshape(2, 2, 4, 512, 128)

    g_other = lax.ppermute(g_top, "y_hi", ring(2, 1))
    lp_far = lax.ppermute(lp_two, "y_hi", ring(2, 1))
    near_one = lax.ppermute(one, ALL_AXES, spread_pairs())
    packed = jnp.concatenate([one, dinv_one])
    pieces = {0: packed}
    right = left = packed
    for d in range(1, 5):
        right = lax.ppermute(right, "z", ring(8, 1))
        if d < 4:
            left = lax.ppermute(left, "z", ring(8, -1))
            if d == 1:
                right, left, near_one, lp_far = lax.optimization_barrier(
                    (right, left, near_one, lp_far)
                )
            pieces[d] = left
        pieces[-d] = right
    pieces[-4], g_other = lax.optimization_barrier((right, g_other))
    gathered_one = gather(near_one)

    def fetch(super_index):
        parts = []
        for part in range(2):
            want = super_index % 4 * 2 + part
            total = jnp.zeros((528, 128), jnp.float32)
            for d, one_piece_here in pieces.items():
                total = jnp.where(want == (z + d) % 8, one_piece_here, total)
            parts.append(total)
        return jnp.concatenate(parts, axis=1)

    par_here = fetch(parent)
    par_there = fetch(parent_two[(1 - h) * 4 + z // 2])
    even = z % 2 == 0
    pair_up = lambda a, b: jnp.where(even, jnp.concatenate([a, b], 1), jnp.concatenate([b, a], 1))
    own_one = pair_up(one, jnp.where(even, pieces[1], pieces[-1])[:512])
    here = parent // 4 == h
    by_lp = lambda cols, lp: jnp.dot(cols[:512], lp, precision=lax.Precision.HIGH)
    from_far = lax.ppermute(by_lp(par_there, lp_far), "y_hi", ring(2, 1))
    folded = two - jnp.where(here, by_lp(par_here, lp_two), from_far)
    folded, g_other = lax.optimization_barrier((folded, g_other))
    near_two = lax.ppermute(folded, ALL_AXES, spread_pairs())

    g_parts = []
    for g in (g_top, g_other):
        g = g.reshape(512, 512)
        g_hi = lax.reduce_precision(g, 8, 7)
        g_parts += [g_hi.astype(jnp.bfloat16), (g - g_hi).astype(jnp.bfloat16)]

    two_sent = jnp.concatenate([two, lp_two])
    two_next = lax.ppermute(two_sent, "z", [(i, i ^ 1) for i in range(8)])
    own_two = pair_up(two, two_next[:512])
    lp_own = pair_up(lp_two, two_next[512:])

    def multiply(gathered, after):
        def part(first_pair, after):
            both = jnp.arange(2, dtype=jnp.int32)
            slots = (first_pair + both) % 4 * 2
            chip, core = chip_and_core((z - slots[:, None] - both[None, :]) % 8)
            codes = chip // 2 * 4 + chip % 2 * 2 + core
            scalars = jnp.concatenate([after[None], codes.reshape(4)]).astype(jnp.int32)
            return product(scalars, g_parts, gathered)

        early = part((z + 4) // 2, after)
        after, early = lax.optimization_barrier((after, early))
        return early, part((z + 4) // 2 + 2, after)

    def sum_over_z(early, late):
        def term(d):
            take = lambda i: early[i] if i < 4 else late[i - 4]
            return jnp.where(even, take((d - 4) % 8), take((d - 3) % 8))

        up = lax.ppermute(term(4), "z", ring(8, 1))
        down = lax.ppermute(term(-3), "z", ring(8, -1))
        up, down, late = lax.optimization_barrier((up, down, late))
        up = lax.ppermute(up + term(3), "z", ring(8, 1))
        down = lax.ppermute(down + term(-2), "z", ring(8, -1))
        up = lax.ppermute(up + term(2), "z", ring(8, 1))
        down = lax.ppermute(down + term(-1), "z", ring(8, -1))
        return lax.ppermute(up + term(1), "z", ring(8, 1)) + down + term(0)

    early, late = multiply(gathered_one, h)
    near_two, early, late = lax.optimization_barrier((near_two, early, late))
    gathered_two = gather(near_two)
    inv_one = sum_over_z(early, late)
    inv_one, own_one, own_two, lp_own, par_there, h_next = lax.optimization_barrier(
        (inv_one, own_one, own_two, lp_own, par_there, h)
    )
    par = jnp.where(here, par_here, lax.ppermute(par_there, "y_hi", ring(2, 1)))
    inv_two = sum_over_z(*multiply(gathered_two, h_next))
    panel_one = jnp.where(keep_one, inv_one.reshape(2, 256, 128), 0.0)
    panel_two = jnp.where(keep_two, inv_two.reshape(2, 256, 128), 0.0)

    dot_t = lambda a, b: lax.dot_general(a, b, (((0,), (0,)), ((), ())), precision=exact)
    scaled = jnp.dot(par[512:], lp_two, precision=exact)
    lp_slab = lax.dynamic_slice_in_dim(lp_own, row * 16, 16, 0)
    quad = dot_t(lp_slab, scaled)
    term_one = dot_t(own_one, inv_one)
    term_par = dot_t(par[:512], inv_two)
    term_two = quad - dot_t(own_two, inv_two) + dot_t(lp_own, term_par)
    terms = jnp.stack([term_one, term_par, term_two]).reshape(3, 16, 16, 128).transpose(1, 0, 2, 3)
    sums = jnp.sum(lax.all_to_all(terms, ROW_AXES, 0, 0), axis=0)
    diag_one = dinv_one - sums[0]
    parent_rows = -(sums[1] + scaled)
    diag_two = dinv_two + sums[2]
    return (panel_one, diag_one, panel_two, parent_rows, diag_two)


def solution(mesh):
    fine = jax.sharding.Mesh(mesh.devices.reshape(4, 2, 2, 2, 8), ALL_AXES)
    tall = P(None, ROW_AXES, COL_AXES)
    flat = P(ROW_AXES, COL_AXES)
    return jax.shard_map(
        local,
        mesh=fine,
        in_specs=(
            P(None, ROW_AXES, None, COL_AXES),
            tall,
            P(),
            flat,
            tall,
            P(None, COL_AXES),
            P(),
            P(),
            flat,
        ),
        out_specs=(tall, flat, tall, flat, flat),
        check_vma=False,
    )
```

```python
import functools

import jax
import jax.numpy as jnp
from jax import lax
from jax.experimental import pallas as pl
from jax.experimental.pallas import tpu as pltpu
from jax.sharding import PartitionSpec as P

ROW_AXES = ("x", "y_lo", "core")
COL_AXES = ("y_hi", "z")
ALL_AXES = ROW_AXES + COL_AXES
exact = lax.Precision.HIGHEST


def split(a):
    hi = a.astype(jnp.bfloat16)
    return hi, (a - hi.astype(jnp.float32)).astype(jnp.bfloat16)


def dot3(a, b):
    f = functools.partial(jnp.dot, preferred_element_type=jnp.float32)
    return f(a[0], b[0]) + (f(a[0], b[1]) + f(a[1], b[0]))


def pair_kernel(sc_ref, *refs):
    g_refs, (a_ref, b_ref, out_ref) = refs[:4], refs[4:]
    h = sc_ref[0]
    acc = None
    for k in range(2):
        half = h if k == 0 else 1 - h
        cols = jnp.concatenate([a_ref[half, 0, 0], b_ref[half, 0, 0]], axis=1)
        term = dot3((g_refs[2 * k][...], g_refs[2 * k + 1][...]), split(cols))
        acc = term if acc is None else acc + term
    out_ref[0] = -acc[:, :128]
    out_ref[1] = -acc[:, 128:]


WHOLE_G = pl.BlockSpec((512, 512), lambda i, sc: (0, 0))
PARAMS = pltpu.CompilerParams(vmem_limit_bytes=40 * 2**20)


def slot_rows(first):
    def place(i, sc):
        code = sc[first + 2 * i]
        return (0, code // 4, code % 4, 0, 0)

    return pl.BlockSpec((2, 1, 1, 512, 128), place)


def product(scalars, g_parts, gathered):
    return pl.pallas_call(
        pair_kernel,
        grid_spec=pltpu.PrefetchScalarGridSpec(
            num_scalar_prefetch=1,
            grid=(2,),
            in_specs=[WHOLE_G] * 4 + [slot_rows(1), slot_rows(2)],
            out_specs=pl.BlockSpec((2, 512, 128), lambda i, sc: (i, 0, 0)),
        ),
        out_shape=jax.ShapeDtypeStruct((4, 512, 128), jnp.float32),
        compiler_params=PARAMS,
        cost_estimate=pl.CostEstimate(
            flops=1_600_000_000, bytes_accessed=7_000_000, transcendentals=0
        ),
    )(scalars, *g_parts, gathered, gathered)


def chip_and_core(shift):
    up = (shift >= 1) & (shift <= 4)
    return (up * (4 - shift) + (1 - up) * (8 - shift)) % 4, 1 - up


def spread_pairs():
    pairs = []
    for i in range(256):
        row, col = divmod(i, 16)
        half, z, h, s = row // 8, row % 8, col // 8, col % 8
        chip, core = chip_and_core((z - s) % 8)
        pairs.append((i, (half * 8 + chip * 2 + int(core)) * 16 + h * 8 + z))
    return pairs


def ring(n, step):
    return [(i, (i + step) % n) for i in range(n)]


def local(g_top, l_one, struct_one, dinv_one, l_two, lp_two, parent_two, pos_two, dinv_two):
    row = lax.axis_index(ROW_AXES)
    h = lax.axis_index("y_hi")
    z = lax.axis_index("z")
    mine = h * 4 + z // 2
    parent = parent_two[mine]

    blocks = jnp.arange(2, dtype=jnp.int32) * 16 + row
    list_one = lax.dynamic_index_in_dim(struct_one, mine, 0, keepdims=False)
    list_parent = lax.dynamic_index_in_dim(struct_one, parent, 0, keepdims=False)
    places = lax.dynamic_index_in_dim(pos_two, mine, 0, keepdims=False)
    picked = jnp.any(places[:, None] == jnp.arange(16)[None, :], axis=0)
    keep_one = jnp.any(list_one[None, :] == blocks[:, None], axis=1)[:, None, None]
    keep_two = jnp.any((list_parent[None, :] == blocks[:, None]) & picked[None, :], axis=1)
    keep_two = keep_two[:, None, None]
    one = jnp.where(keep_one, l_one, 0.0).reshape(512, 128)
    two = jnp.where(keep_two, l_two, 0.0).reshape(512, 128)

    def gather(piece):
        rows = lax.all_gather(piece, ROW_AXES, axis=0, tiled=False)
        return rows.reshape(2, 2, 4, 512, 128)

    g_other = lax.ppermute(g_top, "y_hi", ring(2, 1))
    lp_far = lax.ppermute(lp_two, "y_hi", ring(2, 1))
    near_one = lax.ppermute(one, ALL_AXES, spread_pairs())
    packed = jnp.concatenate([one, dinv_one])
    pieces = {0: packed}
    right = left = packed
    for d in range(1, 5):
        right = lax.ppermute(right, "z", ring(8, 1))
        if d < 4:
            left = lax.ppermute(left, "z", ring(8, -1))
            if d == 1:
                right, left, near_one, lp_far, g_other = lax.optimization_barrier(
                    (right, left, near_one, lp_far, g_other)
                )
            pieces[d] = left
        pieces[-d] = right
    gathered_one = gather(near_one)

    def fetch(super_index):
        parts = []
        for part in range(2):
            want = super_index % 4 * 2 + part
            total = jnp.zeros((528, 128), jnp.float32)
            for d, one_piece_here in pieces.items():
                total = jnp.where(want == (z + d) % 8, one_piece_here, total)
            parts.append(total)
        return jnp.concatenate(parts, axis=1)

    par_here = fetch(parent)
    par_there = fetch(parent_two[(1 - h) * 4 + z // 2])
    even = z % 2 == 0
    pair_up = lambda a, b: jnp.where(even, jnp.concatenate([a, b], 1), jnp.concatenate([b, a], 1))
    own_one = pair_up(one, jnp.where(even, pieces[1], pieces[-1])[:512])
    here = parent // 4 == h
    by_lp = lambda cols, lp: jnp.dot(cols[:512], lp, precision=lax.Precision.HIGH)
    from_far = lax.ppermute(by_lp(par_there, lp_far), "y_hi", ring(2, 1))
    folded = two - jnp.where(here, by_lp(par_here, lp_two), from_far)
    two_sent = jnp.concatenate([two, lp_two])
    folded, g_other, two_sent = lax.optimization_barrier((folded, g_other, two_sent))
    near_two = lax.ppermute(folded, ALL_AXES, spread_pairs())

    g_parts = []
    for g in (g_top, g_other):
        g = g.reshape(512, 512)
        g_hi = lax.reduce_precision(g, 8, 7)
        g_parts += [g_hi.astype(jnp.bfloat16), (g - g_hi).astype(jnp.bfloat16)]

    two_next = lax.ppermute(two_sent, "z", [(i, i ^ 1) for i in range(8)])

    def multiply(gathered, after):
        def part(first_pair, after):
            both = jnp.arange(2, dtype=jnp.int32)
            slots = (first_pair + both) % 4 * 2
            chip, core = chip_and_core((z - slots[:, None] - both[None, :]) % 8)
            codes = chip // 2 * 4 + chip % 2 * 2 + core
            scalars = jnp.concatenate([after[None], codes.reshape(4)]).astype(jnp.int32)
            return product(scalars, g_parts, gathered)

        early = part((z + 4) // 2, after)
        after, early = lax.optimization_barrier((after, early))
        return early, part((z + 4) // 2 + 2, after)

    def sum_over_z(early, late):
        def term(d):
            take = lambda i: early[i] if i < 4 else late[i - 4]
            return jnp.where(even, take((d - 4) % 8), take((d - 3) % 8))

        up = lax.ppermute(term(4), "z", ring(8, 1))
        down = lax.ppermute(term(-3), "z", ring(8, -1))
        up, down, late = lax.optimization_barrier((up, down, late))
        up = lax.ppermute(up + term(3), "z", ring(8, 1))
        down = lax.ppermute(down + term(-2), "z", ring(8, -1))
        up = lax.ppermute(up + term(2), "z", ring(8, 1))
        down = lax.ppermute(down + term(-1), "z", ring(8, -1))
        return lax.ppermute(up + term(1), "z", ring(8, 1)) + down + term(0)

    early, late = multiply(gathered_one, h)
    near_two, early, late, two_next = lax.optimization_barrier(
        (near_two, early, late, two_next)
    )
    gathered_two = gather(near_two)
    own_two = pair_up(two, two_next[:512])
    lp_own = pair_up(lp_two, two_next[512:])
    inv_one = sum_over_z(early, late)
    inv_one, own_one, own_two, lp_own, par_there, h_next = lax.optimization_barrier(
        (inv_one, own_one, own_two, lp_own, par_there, h)
    )
    par = jnp.where(here, par_here, lax.ppermute(par_there, "y_hi", ring(2, 1)))
    inv_two = sum_over_z(*multiply(gathered_two, h_next))
    panel_one = jnp.where(keep_one, inv_one.reshape(2, 256, 128), 0.0)
    panel_two = jnp.where(keep_two, inv_two.reshape(2, 256, 128), 0.0)

    dot_t = lambda a, b: lax.dot_general(a, b, (((0,), (0,)), ((), ())), precision=exact)
    scaled = jnp.dot(par[512:], lp_two, precision=exact)
    lp_slab = lax.dynamic_slice_in_dim(lp_own, row * 16, 16, 0)
    quad = dot_t(lp_slab, scaled)
    term_one = dot_t(own_one, inv_one)
    term_par = dot_t(par[:512], inv_two)
    term_two = quad - dot_t(own_two, inv_two) + dot_t(lp_own, term_par)
    terms = jnp.stack([term_one, term_par, term_two]).reshape(3, 16, 16, 128).transpose(1, 0, 2, 3)
    sums = jnp.sum(lax.all_to_all(terms, ROW_AXES, 0, 0), axis=0)
    diag_one = dinv_one - sums[0]
    parent_rows = -(sums[1] + scaled)
    diag_two = dinv_two + sums[2]
    return (panel_one, diag_one, panel_two, parent_rows, diag_two)


def solution(mesh):
    fine = jax.sharding.Mesh(mesh.devices.reshape(4, 2, 2, 2, 8), ALL_AXES)
    tall = P(None, ROW_AXES, COL_AXES)
    flat = P(ROW_AXES, COL_AXES)
    return jax.shard_map(
        local,
        mesh=fine,
        in_specs=(
            P(None, ROW_AXES, None, COL_AXES),
            tall,
            P(),
            flat,
            tall,
            P(None, COL_AXES),
            P(),
            P(),
            flat,
        ),
        out_specs=(tall, flat, tall, flat, flat),
        check_vma=False,
    )
```
